512 devices in a mesh: rows: 64 (over y_hi, z, core), cols: 8 (over x, y_lo).
Axes of the slice: x: 4, y: 4 (y_hi: 2, y_lo: 2; y = y_hi * 2 + y_lo), z: 16, core: 2. Of those that a mesh axis runs over, the one named last changes fastest.
Arguments:
- low_frames: bfloat16 [256, 128, 128], P('rows', 'cols'), may hold values from -6 to 6
- conv_weight: bfloat16 [3456, 128], replicated, may hold values from -0.109375 to 0.109375
- attn_in: bfloat16 [128, 384], replicated, may hold values from -2 to 2
- attn_out: bfloat16 [128, 128], replicated, may hold values from -0.5 to 0.5
Outputs:
- refined: bfloat16 [1024, 512, 128], P('rows', 'cols')
The draws below stay inside these ranges and needn't reach their ends.
All inputs are finite; a program needn't handle non-finite values.
Results may differ from the reference program's by a relative error of at most 0.0068.
Values may be sent and summed in bfloat16 or wider, within the bound.
A program may use at most 64 MiB of HBM per device.

```python
import jax
import jax.numpy as jnp
from jax import lax

C = 128
HEADS = 2
BANDS = 2
LR = 4
LC = 16
F = 32
N_COLS = 8


def draw_low_frames(key, part):
    key = jax.random.fold_in(key, 11)
    subkeys = jax.random.split(key, 1)
    shape = (BANDS * F * LR, LC * N_COLS, C)
    return jnp.clip(jax.random.normal(subkeys[0], shape, jnp.float32), -6.0, 6.0).astype(jnp.bfloat16)


def draw_attn_in(key, part):
    key = jax.random.fold_in(key, 7)
    subkeys = jax.random.split(key, 3)
    scale = 1.0 / jnp.sqrt(jnp.float32(C))
    basis = jnp.clip(jax.random.normal(subkeys[0], (C, C), jnp.float32), -4.0, 4.0) * scale
    keyed = jnp.clip(jax.random.normal(subkeys[1], (C, C), jnp.float32), -4.0, 4.0) * scale
    values = jnp.clip(jax.random.normal(subkeys[2], (C, C), jnp.float32), -4.0, 4.0) * scale
    queries = basis
    return jnp.concatenate([queries, keyed, values], axis=1).astype(jnp.bfloat16)


def scatter_about(rng, shape, scale, bound, kind=jnp.bfloat16):
    values = scale * jax.random.normal(rng, shape, jnp.float32)
    return jnp.clip(values, min=-bound, max=bound).astype(kind)


def setup_inputs(seed: int = 0) -> dict:
    key_list = jax.random.split(jax.random.key(seed), 5)
    return {
        "low_frames": draw_low_frames(jax.random.fold_in(key_list[4], 71), 0),
        "conv_weight": scatter_about(key_list[1], (27 * C, C), (27 * C) ** -0.5, 0.109375),
        "attn_in": draw_attn_in(jax.random.fold_in(key_list[4], 71), 0),
        "attn_out": scatter_about(key_list[3], (C, C), C ** -0.5, 0.5),
    }


def upsample_axis(values, axis):
    count = values.shape[axis] - 2

    def sliced(begin, end):
        return lax.slice_in_dim(values, begin, end, axis=axis)
    before = sliced(0, count)
    centre = sliced(1, count + 1)
    behind = sliced(2, count + 2)
    phases = jnp.stack([0.375 * before + 0.625 * centre, 0.125 * before + 0.875 * centre, 0.875 * centre + 0.125 * behind, 0.625 * centre + 0.375 * behind], axis=axis + 1)
    target = list(centre.shape)
    target[axis] = 4 * count
    middle = phases.reshape(target)
    opening = 0.625 * sliced(0, 1) + 0.375 * sliced(1, 2)
    closing = 0.375 * sliced(count, count + 1) + 0.625 * sliced(count + 1, count + 2)
    return jnp.concatenate([opening, middle, closing], axis=axis)

def reference(low_frames, conv_weight, attn_in, attn_out):
    width = LC * N_COLS
    frames = low_frames.reshape(BANDS, F, LR, width, C)
    frames = jnp.transpose(frames, (1, 0, 2, 3, 4)).reshape(F, BANDS * LR, width, C).astype(jnp.float32)
    padded = jnp.pad(frames, ((0, 0), (1, 1), (1, 1), (0, 0)), mode='edge')
    upsampled = upsample_axis(upsample_axis(padded, 1), 2)[:, 1:-1, 1:-1, :].astype(jnp.bfloat16)
    rows_high = upsampled.shape[1]
    cols_high = upsampled.shape[2]
    bordered = jnp.pad(upsampled, ((1, 1), (1, 1), (1, 1), (0, 0)))
    taps = conv_weight.reshape(9, 3 * C, C)

    def conv_frame(index):
        slab = lax.dynamic_slice_in_dim(bordered, index, 3, 0)
        total = jnp.zeros((rows_high * cols_high, C), jnp.float32)
        for tap_t in range(3):
            for tap_y in range(3):
                window = jnp.concatenate([slab[tap_t, tap_y:tap_y + rows_high, offset:offset + cols_high] for offset in range(3)], axis=-1).reshape(-1, 3 * C)
                total = total + jnp.dot(window, taps[3 * tap_t + tap_y], preferred_element_type=jnp.float32)
        return total.reshape(rows_high, cols_high, C)
    convolved = lax.map(conv_frame, jnp.arange(F))
    features = (upsampled.astype(jnp.float32) + jax.nn.silu(convolved)).astype(jnp.bfloat16)
    head_size = C // HEADS

    def attend_row(index):
        row_block = lax.dynamic_index_in_dim(features, index, 1, keepdims=False)
        projected = jnp.dot(row_block.reshape(-1, C), attn_in, preferred_element_type=jnp.float32).astype(jnp.bfloat16)
        projected = projected.reshape(F, cols_high, 3, HEADS, head_size).astype(jnp.float32)
        scores = jnp.einsum('fwhd,gwhd->whfg', projected[:, :, 0], projected[:, :, 1]) / jnp.sqrt(jnp.float32(head_size))
        scores = scores - lax.optimization_barrier(jnp.max(scores, axis=-1, keepdims=True))
        expo = jnp.exp(scores)
        weights = (expo / lax.optimization_barrier(jnp.sum(expo, axis=-1, keepdims=True))).astype(jnp.bfloat16)
        context = jnp.einsum('whfg,gwhd->fwhd', weights.astype(jnp.float32), projected[:, :, 2]).astype(jnp.bfloat16)
        output = jnp.dot(context.reshape(-1, C), attn_out, preferred_element_type=jnp.float32)
        return (row_block.reshape(-1, C).astype(jnp.float32) + output).astype(jnp.bfloat16).reshape(F, cols_high, C)
    refined = lax.map(attend_row, jnp.arange(rows_high))
    refined = refined.reshape(BANDS, 4 * LR, F, cols_high, C)
    return jnp.transpose(refined, (0, 2, 1, 3, 4)).reshape(BANDS * F * 4 * LR, cols_high, C)
```

```python
import jax
import jax.numpy as jnp
from jax import lax
from jax.experimental import pallas as pl
from jax.experimental.pallas import tpu as pltpu
from jax.sharding import PartitionSpec as P

MESH = pl.DeviceIdType.MESH
F32 = jnp.float32
BF16 = jnp.bfloat16
FRAMES = 32
CH = 128
HALVES = 2
OFFSETS = [s for d in range(1, 17) for s in ((d,) if d == 16 else (d, 32 - d))]
TAPS = ((0.375, 0.625), (0.125, 0.875), (0.875, 0.125), (0.625, 0.375))


def lerp(weights, a, b):
    return weights[0] * a + weights[1] * b


def spread(x):
    out = [lerp(TAPS[3], x[0], x[1])]
    for k in range(1, len(x) - 1):
        out.append(lerp(TAPS[0], x[k - 1], x[k]))
        out.append(lerp(TAPS[1], x[k - 1], x[k]))
        out.append(lerp(TAPS[2], x[k], x[k + 1]))
        out.append(lerp(TAPS[3], x[k], x[k + 1]))
    out.append(lerp(TAPS[0], x[-2], x[-1]))
    return out


def kernel(
    low_hbm, w_hbm, ain_hbm, aout_hbm, out,
    low, w, ain, aout, edge, hal, hband, ext, extw, got, gf, u, rf, snd,
    ld_sem, h_send, h_recv, in_send, in_recv, o_send, o_recv,
):
    place = lax.axis_index("rows")
    col = lax.axis_index("cols")
    band = place // FRAMES
    me = place % FRAMES
    base = band * FRAMES
    other = (1 - band) * FRAMES + me
    left = (col + 7) % 8
    right = (col + 1) % 8

    def load(k, src, dst):
        cp = pltpu.make_async_copy(src, dst, ld_sem.at[k])
        cp.start()
        return cp

    load_low = load(0, low_hbm, low)
    load_w = load(1, w_hbm, w)
    load_ain = load(2, ain_hbm, ain)
    load_aout = load(3, aout_hbm, aout)

    bar = pltpu.get_barrier_semaphore()
    near = ((place, left), (place, right), (other, col), (other, left), (other, right))
    for target in near:
        pl.semaphore_signal(bar, inc=1, device_id=target, device_id_type=MESH)
    for s in OFFSETS:
        pl.semaphore_signal(
            bar, inc=1, device_id=(base + (me + s) % FRAMES, col), device_id_type=MESH
        )
    load_low.wait()
    edge[0] = low[:, 0, :]
    edge[1] = low[:, 15, :]
    pl.semaphore_wait(bar, FRAMES - 1 + len(near))

    edge_row = (1 - band) * 3
    sends = (
        (edge.at[1], hal.at[0], (place, right)),
        (edge.at[0], hal.at[1], (place, left)),
        (edge.at[1], hal.at[2], (other, right)),
        (edge.at[0], hal.at[3], (other, left)),
        (low.at[edge_row], hband, (other, col)),
    )
    rims = []
    for k, (src, dst, target) in enumerate(sends):
        cp = pltpu.make_async_remote_copy(
            src_ref=src, dst_ref=dst, send_sem=h_send.at[k], recv_sem=h_recv.at[k],
            device_id=target, device_id_type=MESH,
        )
        cp.start()
        rims.append(cp)
    mine = low[...].astype(F32)
    ext[1:5, 1:17] = mine
    for cp in rims:
        cp.wait_recv()
    first = col == 0
    last = col == 7
    ext[1:5, 0:1] = jnp.where(first, mine[:, 0:1], hal[0].astype(F32).reshape(4, 1, CH))
    ext[1:5, 17:18] = jnp.where(last, mine[:, 15:16], hal[1].astype(F32).reshape(4, 1, CH))
    across = hband[...].astype(F32)
    cl = hal[2].astype(F32)
    cr = hal[3].astype(F32)
    upper = band == 0
    cl = jnp.where(upper, cl[0:1], cl[3:4])
    cr = jnp.where(upper, cr[0:1], cr[3:4])
    cl = jnp.where(first, across[0:1], cl)
    cr = jnp.where(last, across[15:16], cr)
    fill_row = jnp.where(upper, 5, 0)
    same_row = jnp.where(upper, 0, 5)
    copy_row = jnp.where(upper, 1, 4)
    ext[fill_row, 1:17] = across
    ext[fill_row, 0:1] = cl
    ext[fill_row, 17:18] = cr
    ext[same_row] = ext[copy_row]
    for j in range(8):
        extw[:, j] = ext[:, 2 * j : 2 * j + 4].astype(BF16)

    for s in OFFSETS:
        slot = (me + s) % FRAMES
        pltpu.make_async_remote_copy(
            src_ref=extw.at[pl.ds(slot // 8, 3), slot % 8], dst_ref=got.at[me],
            send_sem=in_send, recv_sem=in_recv,
            device_id=(base + slot, col), device_id_type=MESH,
        ).start()
    got[me] = extw[pl.ds(me // 8, 3), me % 8]
    pltpu.make_async_copy(got.at[pl.ds(0, 31)], got.at[pl.ds(0, 31)], in_recv).wait()

    for f in range(FRAMES):
        for k in range(3):
            gf[12 * f + 4 * k : 12 * f + 4 * k + 4] = got[f, k].astype(F32)
    grid = [[gf[pl.ds(4 * k + c, FRAMES, stride=12)] for c in range(4)] for k in range(3)]
    columns = [spread([grid[k][c] for k in range(3)]) for c in range(4)]
    patch_row = me // 8
    patch_col = me % 8
    keep_top = jnp.where(upper & (patch_row == 0), 0.0, 1.0).astype(F32)
    keep_bottom = jnp.where((band == 1) & (patch_row == 3), 0.0, 1.0).astype(F32)
    keep_left = jnp.where(first & (patch_col == 0), 0.0, 1.0).astype(F32)
    keep_right = jnp.where(last & (patch_col == 7), 0.0, 1.0).astype(F32)
    for y in range(6):
        row = spread([columns[c][y] for c in range(4)])
        for x in range(10):
            value = row[x]
            if y == 0:
                value = value * keep_top
            if y == 5:
                value = value * keep_bottom
            if x == 0:
                value = value * keep_left
            if x == 9:
                value = value * keep_right
            u[y, x] = value.astype(BF16)

    load_w.wait()
    load_ain.wait()
    load_aout.wait()

    pixels = 16
    rows = pixels * FRAMES
    frame_id = lax.broadcasted_iota(jnp.int32, (rows, CH), 0) % FRAMES
    lane = lax.broadcasted_iota(jnp.int32, (128, CH), 1)
    head0 = (lane < 64).astype(F32).astype(BF16)
    head1 = (lane >= 64).astype(F32).astype(BF16)
    ones = jnp.concatenate([head0, head1], axis=0)
    s_row = lax.broadcasted_iota(jnp.int32, (128, 256), 0) // FRAMES
    s_lane = lax.broadcasted_iota(jnp.int32, (128, 256), 1) % 128 // FRAMES
    same_pixel = s_row == s_lane

    for h in range(HALVES):
        lhs = jnp.concatenate(
            [
                u[2 * h + dy : 2 * h + dy + 2, dx : dx + 8].reshape(rows, CH)
                for dy in range(3)
                for dx in range(3)
            ],
            axis=1,
        )
        w01 = jnp.concatenate([w[0:1152], w[1152:2304]], axis=1)
        y01 = jnp.dot(lhs, w01, preferred_element_type=F32)
        y2 = jnp.dot(lhs, w[2304:3456], preferred_element_type=F32)
        before = jnp.where(frame_id == 0, 0.0, pltpu.roll(y01[:, :CH], 1, 0))
        after = jnp.where(frame_id == FRAMES - 1, 0.0, pltpu.roll(y2, rows - 1, 0))
        total = before + y01[:, CH:] + after
        centre = u[2 * h + 1 : 2 * h + 3, 1:9].reshape(rows, CH).astype(F32)
        feat = (centre + total / (1.0 + jnp.exp(-total))).astype(BF16)
        proj = jnp.dot(feat, ain[...], preferred_element_type=F32).astype(BF16)
        for g in range(4):
            part = proj[128 * g : 128 * g + 128]
            q = part[:, :CH]
            k = part[:, CH : 2 * CH]
            v = part[:, 2 * CH :]
            keys = jnp.concatenate([k * head0, k * head1], axis=0)
            scores = lax.dot_general(
                q, keys, (((1,), (1,)), ((), ())), preferred_element_type=F32
            )
            scores = jnp.where(same_pixel, scores * 0.125, -1e30)
            m0 = jnp.max(scores[:, :128], axis=1, keepdims=True)
            m1 = jnp.max(scores[:, 128:], axis=1, keepdims=True)
            expo = jnp.concatenate(
                [jnp.exp(scores[:, :128] - m0), jnp.exp(scores[:, 128:] - m1)], axis=1
            ).astype(BF16)
            values = jnp.concatenate([v * head0, v * head1], axis=0)
            summed = jnp.dot(
                expo, jnp.concatenate([values, ones], axis=1), preferred_element_type=F32
            )
            context = (summed[:, :CH] / summed[:, CH:]).astype(BF16)
            output = jnp.dot(context, aout[...], preferred_element_type=F32)
            rf[128 * g : 128 * g + 128] = feat[128 * g : 128 * g + 128].astype(F32) + output
        for f in range(FRAMES):
            snd[h, f] = rf[pl.ds(f, pixels, stride=FRAMES)].astype(BF16)
        for s in OFFSETS:
            frame = (me + s) % FRAMES
            pltpu.make_async_remote_copy(
                src_ref=snd.at[h, frame], dst_ref=out.at[me, h],
                send_sem=o_send.at[h], recv_sem=o_recv.at[h],
                device_id=(base + frame, col), device_id_type=MESH,
            ).start()
        out[me, h] = snd[h, me]

    for cp in rims:
        cp.wait_send()
    pltpu.make_async_copy(got.at[pl.ds(0, 31)], got.at[pl.ds(0, 31)], in_send).wait()
    for h in range(HALVES):
        block = snd.at[h, pl.ds(0, 31)]
        pltpu.make_async_copy(block, block, o_send.at[h]).wait()
        pltpu.make_async_copy(block, block, o_recv.at[h]).wait()


def local(low_frames, conv_weight, attn_in, attn_out):
    vmem = pltpu.VMEM
    dma = pltpu.SemaphoreType.DMA
    patches = pl.pallas_call(
        kernel,
        out_shape=jax.ShapeDtypeStruct((FRAMES, HALVES, 16, CH), BF16),
        in_specs=[pl.BlockSpec(memory_space=pl.ANY)] * 4,
        out_specs=pl.BlockSpec(memory_space=pltpu.VMEM),
        scratch_shapes=[
            vmem((4, 16, CH), BF16),
            vmem((27 * CH, CH), BF16),
            vmem((CH, 3 * CH), BF16),
            vmem((CH, CH), BF16),
            vmem((2, 4, CH), BF16),
            vmem((4, 4, CH), BF16),
            vmem((16, CH), BF16),
            vmem((6, 24, CH), F32),
            vmem((6, 8, 4, CH), BF16),
            vmem((FRAMES, 3, 4, CH), BF16),
            vmem((FRAMES * 12, CH), F32),
            vmem((6, 10, FRAMES, CH), BF16),
            vmem((16 * FRAMES, CH), F32),
            vmem((HALVES, FRAMES, 16, CH), BF16),
            dma((4,)),
            dma((5,)),
            dma((5,)),
            dma,
            dma,
            dma((HALVES,)),
            dma((HALVES,)),
        ],
        compiler_params=pltpu.CompilerParams(
            collective_id=0, has_side_effects=True, vmem_limit_bytes=32 * 1024 * 1024
        ),
    )(low_frames, conv_weight, attn_in, attn_out)
    blocks = patches.reshape(4, 8, 4, 8, CH)
    return jnp.transpose(blocks, (0, 2, 1, 3, 4)).reshape(16, 64, CH)


def solution(mesh):
    in_specs = (P("rows", "cols", None), P(), P(), P())
    out_specs = P("rows", "cols", None)
    return jax.shard_map(local, mesh=mesh, in_specs=in_specs, out_specs=out_specs, check_vma=False)
```

```python
import jax
import jax.numpy as jnp
from jax import lax
from jax.experimental import pallas as pl
from jax.experimental.pallas import tpu as pltpu
from jax.sharding import PartitionSpec as P

MESH = pl.DeviceIdType.MESH
F32 = jnp.float32
BF16 = jnp.bfloat16
FRAMES = 32
CH = 128
HALVES = 2
OFFSETS = [s for d in range(16, 0, -1) for s in ((d,) if d == 16 else (d, 32 - d))]
TAPS = ((0.375, 0.625), (0.125, 0.875), (0.875, 0.125), (0.625, 0.375))


def lerp(weights, a, b):
    return weights[0] * a + weights[1] * b


def spread(x):
    out = [lerp(TAPS[3], x[0], x[1])]
    for k in range(1, len(x) - 1):
        out.append(lerp(TAPS[0], x[k - 1], x[k]))
        out.append(lerp(TAPS[1], x[k - 1], x[k]))
        out.append(lerp(TAPS[2], x[k], x[k + 1]))
        out.append(lerp(TAPS[3], x[k], x[k + 1]))
    out.append(lerp(TAPS[0], x[-2], x[-1]))
    return out


def patch_of(index, band):
    rest = index - 14
    depth = jnp.where(
        index < 8, 0, jnp.where(index < 14, 1 + (index - 8) // 2, 1 + rest // 6)
    )
    column = jnp.where(
        index < 8, index, jnp.where(index < 14, 7 * (index % 2), 1 + rest % 6)
    )
    return jnp.where(band == 0, 3 - depth, depth), column


def kernel(
    low_hbm, w_hbm, ain_hbm, aout_hbm, out,
    low, w, ain, aout, edge, ext, extw, got, halo, gf, gh, u, rf, snd,
    ld_sem, in_send, in_recv, h_send, h_recv, o_send, o_recv,
):
    place = lax.axis_index("rows")
    col = lax.axis_index("cols")
    band = place // FRAMES
    me = place % FRAMES
    base = band * FRAMES
    across = (1 - band) * FRAMES
    left = (col + 7) % 8
    right = (col + 1) % 8
    patch_row, patch_col = patch_of(me, band)
    patch = patch_row * 8 + patch_col
    border = jnp.where(band == 0, 3, 0)
    at_border = patch_row == border
    at_left = patch_col == 0
    at_right = patch_col == 7

    def load(k, src, dst):
        cp = pltpu.make_async_copy(src, dst, ld_sem.at[k])
        cp.start()
        return cp

    load_low = load(0, low_hbm, low)
    load_w = load(1, w_hbm, w)
    load_ain = load(2, ain_hbm, ain)
    load_aout = load(3, aout_hbm, aout)

    bar = pltpu.get_barrier_semaphore()

    def tell(row, column):
        pl.semaphore_signal(bar, inc=1, device_id=(row, column), device_id_type=MESH)

    def tell_ring(ring, column):
        def one(f, _):
            tell(ring + f, column)
            return _

        lax.fori_loop(0, FRAMES, one, 0)

    for s in OFFSETS:
        tell(base + (me + s) % FRAMES, col)

    @pl.when(at_left)
    def _():
        tell_ring(base, left)

    @pl.when(at_right)
    def _():
        tell_ring(base, right)

    @pl.when(at_border)
    def _():
        tell_ring(across, col)

    @pl.when(at_border & at_left)
    def _():
        tell_ring(across, left)

    @pl.when(at_border & at_right)
    def _():
        tell_ring(across, right)

    load_low.wait()
    mine = low[...].astype(F32)
    edge[0] = low[:, 0, :]
    edge[1] = low[:, 15, :]
    ext[1:5, 1:17] = mine
    ext[1:5, 0:1] = mine[:, 0:1]
    ext[1:5, 17:18] = mine[:, 15:16]
    ext[0] = ext[1]
    ext[5] = ext[4]
    for j in range(8):
        extw[:, j] = ext[:, 2 * j : 2 * j + 4].astype(BF16)
    pl.semaphore_wait(bar, FRAMES - 1 + 18)

    for s in OFFSETS:
        to = (me + s) % FRAMES
        r, j = patch_of(to, band)
        pltpu.make_async_remote_copy(
            src_ref=extw.at[pl.ds(r, 3), j], dst_ref=got.at[me],
            send_sem=in_send, recv_sem=in_recv,
            device_id=(base + to, col), device_id_type=MESH,
        ).start()

    def rim(src, kind, to, column):
        pltpu.make_async_remote_copy(
            src_ref=src, dst_ref=halo.at[kind, me], send_sem=h_send, recv_sem=h_recv.at[kind],
            device_id=(to, column), device_id_type=MESH,
        ).start()

    for to in (0, 8, 10, 12):
        rim(edge.at[1], 0, base + to, right)
    for to in (7, 9, 11, 13):
        rim(edge.at[0], 1, base + to, left)
    for to in range(8):
        rim(extw.at[border + 1, to], 2, across + to, col)
    rim(edge.at[1], 3, across, right)
    rim(edge.at[0], 4, across + 7, left)
    got[me] = extw[pl.ds(patch_row, 3), patch_col]

    pltpu.make_async_copy(got.at[pl.ds(0, 31)], got.at[pl.ds(0, 31)], in_recv).wait()
    for f in range(FRAMES):
        for k in range(3):
            gf[12 * f + 4 * k : 12 * f + 4 * k + 4] = got[f, k].astype(F32)

    def take(kind):
        pltpu.make_async_copy(halo.at[kind], halo.at[kind], h_recv.at[kind]).wait()
        for f in range(FRAMES):
            gh[4 * f : 4 * f + 4] = halo[kind, f].astype(F32)

    border_row = jnp.where(band == 0, 2, 0)
    other_row = jnp.where(band == 0, 0, 3)

    @pl.when(at_border)
    def _():
        take(2)
        for c in range(4):
            gf[pl.ds(4 * border_row + c, FRAMES, stride=12)] = gh[pl.ds(c, FRAMES, stride=4)]

    def side(kind, c, inside):
        take(kind)

        @pl.when(inside)
        def _():
            for k in range(3):
                r = jnp.clip(patch_row - 1 + k, 0, 3)
                gf[pl.ds(4 * k + c, FRAMES, stride=12)] = gh[pl.ds(r, FRAMES, stride=4)]

        @pl.when(at_border)
        def _():
            take(kind + 3)

            @pl.when(inside)
            def _():
                gf[pl.ds(4 * border_row + c, FRAMES, stride=12)] = gh[
                    pl.ds(other_row, FRAMES, stride=4)
                ]

    @pl.when(at_left)
    def _():
        side(0, 0, col > 0)

    @pl.when(at_right)
    def _():
        side(1, 3, col < 7)

    grid = [[gf[pl.ds(4 * k + c, FRAMES, stride=12)] for c in range(4)] for k in range(3)]
    columns = [spread([grid[k][c] for k in range(3)]) for c in range(4)]
    keep_top = jnp.where((band == 0) & (patch_row == 0), 0.0, 1.0).astype(F32)
    keep_bottom = jnp.where((band == 1) & (patch_row == 3), 0.0, 1.0).astype(F32)
    keep_left = jnp.where((col == 0) & at_left, 0.0, 1.0).astype(F32)
    keep_right = jnp.where((col == 7) & at_right, 0.0, 1.0).astype(F32)
    for y in range(6):
        row = spread([columns[c][y] for c in range(4)])
        for x in range(10):
            value = row[x]
            if y == 0:
                value = value * keep_top
            if y == 5:
                value = value * keep_bottom
            if x == 0:
                value = value * keep_left
            if x == 9:
                value = value * keep_right
            u[y, x] = value.astype(BF16)

    load_w.wait()
    load_ain.wait()
    load_aout.wait()

    pixels = 16
    rows = pixels * FRAMES
    frame_id = lax.broadcasted_iota(jnp.int32, (rows, CH), 0) % FRAMES
    lane = lax.broadcasted_iota(jnp.int32, (128, CH), 1)
    head0 = (lane < 64).astype(F32).astype(BF16)
    head1 = (lane >= 64).astype(F32).astype(BF16)
    ones = jnp.concatenate([head0, head1], axis=0)
    s_row = lax.broadcasted_iota(jnp.int32, (128, 256), 0) // FRAMES
    s_lane = lax.broadcasted_iota(jnp.int32, (128, 256), 1) % 128 // FRAMES
    same_pixel = s_row == s_lane

    for h in range(HALVES):
        lhs = jnp.concatenate(
            [
                u[2 * h + dy : 2 * h + dy + 2, dx : dx + 8].reshape(rows, CH)
                for dy in range(3)
                for dx in range(3)
            ],
            axis=1,
        )
        w01 = jnp.concatenate([w[0:1152], w[1152:2304]], axis=1)
        y01 = jnp.dot(lhs, w01, preferred_element_type=F32)
        y2 = jnp.dot(lhs, w[2304:3456], preferred_element_type=F32)
        before = jnp.where(frame_id == 0, 0.0, pltpu.roll(y01[:, :CH], 1, 0))
        after = jnp.where(frame_id == FRAMES - 1, 0.0, pltpu.roll(y2, rows - 1, 0))
        total = before + y01[:, CH:] + after
        centre = u[2 * h + 1 : 2 * h + 3, 1:9].reshape(rows, CH).astype(F32)
        feat = (centre + total / (1.0 + jnp.exp(-total))).astype(BF16)
        proj = jnp.dot(feat, ain[...], preferred_element_type=F32).astype(BF16)
        for g in range(4):
            part = proj[128 * g : 128 * g + 128]
            q = part[:, :CH]
            k = part[:, CH : 2 * CH]
            v = part[:, 2 * CH :]
            keys = jnp.concatenate([k * head0, k * head1], axis=0)
            scores = lax.dot_general(
                q, keys, (((1,), (1,)), ((), ())), preferred_element_type=F32
            )
            scores = jnp.where(same_pixel, scores * 0.125, -1e30)
            m0 = jnp.max(scores[:, :128], axis=1, keepdims=True)
            m1 = jnp.max(scores[:, 128:], axis=1, keepdims=True)
            expo = jnp.concatenate(
                [jnp.exp(scores[:, :128] - m0), jnp.exp(scores[:, 128:] - m1)], axis=1
            ).astype(BF16)
            values = jnp.concatenate([v * head0, v * head1], axis=0)
            summed = jnp.dot(
                expo, jnp.concatenate([values, ones], axis=1), preferred_element_type=F32
            )
            context = (summed[:, :CH] / summed[:, CH:]).astype(BF16)
            output = jnp.dot(context, aout[...], preferred_element_type=F32)
            rf[128 * g : 128 * g + 128] = feat[128 * g : 128 * g + 128].astype(F32) + output
        for f in range(FRAMES):
            snd[h, f] = rf[pl.ds(f, pixels, stride=FRAMES)].astype(BF16)
        for s in OFFSETS:
            frame = (me + s) % FRAMES
            pltpu.make_async_remote_copy(
                src_ref=snd.at[h, frame], dst_ref=out.at[patch, h],
                send_sem=o_send.at[h], recv_sem=o_recv.at[h],
                device_id=(base + frame, col), device_id_type=MESH,
            ).start()
        out[patch, h] = snd[h, me]

    sent = halo.at[0, pl.ds(0, 18)]
    pltpu.make_async_copy(sent, sent, h_send).wait()
    pltpu.make_async_copy(got.at[pl.ds(0, 31)], got.at[pl.ds(0, 31)], in_send).wait()
    for h in range(HALVES):
        block = snd.at[h, pl.ds(0, 31)]
        pltpu.make_async_copy(block, block, o_send.at[h]).wait()
        pltpu.make_async_copy(block, block, o_recv.at[h]).wait()


def local(low_frames, conv_weight, attn_in, attn_out):
    vmem = pltpu.VMEM
    dma = pltpu.SemaphoreType.DMA
    patches = pl.pallas_call(
        kernel,
        out_shape=jax.ShapeDtypeStruct((FRAMES, HALVES, 16, CH), BF16),
        in_specs=[pl.BlockSpec(memory_space=pl.ANY)] * 4,
        out_specs=pl.BlockSpec(memory_space=pltpu.VMEM),
        scratch_shapes=[
            vmem((4, 16, CH), BF16),
            vmem((27 * CH, CH), BF16),
            vmem((CH, 3 * CH), BF16),
            vmem((CH, CH), BF16),
            vmem((2, 4, CH), BF16),
            vmem((6, 24, CH), F32),
            vmem((6, 8, 4, CH), BF16),
            vmem((FRAMES, 3, 4, CH), BF16),
            vmem((5, FRAMES, 4, CH), BF16),
            vmem((FRAMES * 12, CH), F32),
            vmem((FRAMES * 4, CH), F32),
            vmem((6, 10, FRAMES, CH), BF16),
            vmem((16 * FRAMES, CH), F32),
            vmem((HALVES, FRAMES, 16, CH), BF16),
            dma((4,)),
            dma,
            dma,
            dma,
            dma((5,)),
            dma((HALVES,)),
            dma((HALVES,)),
        ],
        compiler_params=pltpu.CompilerParams(
            collective_id=0, has_side_effects=True, vmem_limit_bytes=56 * 1024 * 1024
        ),
    )(low_frames, conv_weight, attn_in, attn_out)
    blocks = patches.reshape(4, 8, 4, 8, CH)
    return jnp.transpose(blocks, (0, 2, 1, 3, 4)).reshape(16, 64, CH)


def solution(mesh):
    in_specs = (P("rows", "cols", None), P(), P(), P())
    out_specs = P("rows", "cols", None)
    return jax.shard_map(local, mesh=mesh, in_specs=in_specs, out_specs=out_specs, check_vma=False)
```

```python
import jax
import jax.numpy as jnp
from jax import lax
from jax.experimental import pallas as pl
from jax.experimental.pallas import tpu as pltpu
from jax.sharding import PartitionSpec as P

MESH = pl.DeviceIdType.MESH
F32 = jnp.float32
BF16 = jnp.bfloat16
FRAMES = 32
EARLY = 16
GROUP_OFFSETS = [s for d in range(8, 0, -1) for s in ((d,) if d == 8 else (d, 16 - d))]
ACROSS_OFFSETS = [0] + GROUP_OFFSETS[::-1]
CH = 128
PIECES = ((0, 1), (1, 4))
OFFSETS = [s for d in range(16, 0, -1) for s in ((d,) if d == 16 else (d, 32 - d))]
TAPS = ((0.375, 0.625), (0.125, 0.875), (0.875, 0.125), (0.625, 0.375))


def lerp(weights, a, b):
    return weights[0] * a + weights[1] * b


def spread(x):
    out = [lerp(TAPS[3], x[0], x[1])]
    for k in range(1, len(x) - 1):
        out.append(lerp(TAPS[0], x[k - 1], x[k]))
        out.append(lerp(TAPS[1], x[k - 1], x[k]))
        out.append(lerp(TAPS[2], x[k], x[k + 1]))
        out.append(lerp(TAPS[3], x[k], x[k + 1]))
    out.append(lerp(TAPS[0], x[-2], x[-1]))
    return out


def patch_of(index, band):
    rest = index - 14
    depth = jnp.where(
        index < 8, 0, jnp.where(index < 14, 1 + (index - 8) // 2, 1 + rest // 6)
    )
    column = jnp.where(
        index < 8, index, jnp.where(index < 14, 7 * (index % 2), 1 + rest % 6)
    )
    return jnp.where(band == 0, 3 - depth, depth), column


def kernel(
    low_hbm, w_hbm, ain_hbm, aout_hbm, out,
    low, w, ain, aout, edge, ext, extw, got, halo, gf, gh, u, rf, snd,
    ld_sem, in_send, in_recv, h_send, h_recv, o_send, o_recv,
):
    place = lax.axis_index("rows")
    col = lax.axis_index("cols")
    band = place // FRAMES
    me = place % FRAMES
    base = band * FRAMES
    across = (1 - band) * FRAMES
    left = (col + 7) % 8
    right = (col + 1) % 8
    patch_row, patch_col = patch_of(me, band)
    patch = patch_row * 8 + patch_col
    border = jnp.where(band == 0, 3, 0)
    at_border = patch_row == border
    at_left = patch_col == 0
    at_right = patch_col == 7

    def load(k, src, dst):
        cp = pltpu.make_async_copy(src, dst, ld_sem.at[k])
        cp.start()
        return cp

    load_low = load(0, low_hbm, low)
    load_w = load(1, w_hbm, w)
    load_ain = load(2, ain_hbm, ain)
    load_aout = load(3, aout_hbm, aout)

    bar = pltpu.get_barrier_semaphore()

    def tell(row, column):
        pl.semaphore_signal(bar, inc=1, device_id=(row, column), device_id_type=MESH)

    def tell_ring(ring, column):
        def one(f, _):
            tell(ring + f, column)
            return _

        lax.fori_loop(0, FRAMES, one, 0)

    for s in OFFSETS:
        tell(base + (me + s) % FRAMES, col)

    @pl.when(at_left)
    def _():
        tell_ring(base, left)

    @pl.when(at_right)
    def _():
        tell_ring(base, right)

    @pl.when(at_border)
    def _():
        tell_ring(across, col)

    @pl.when(at_border & at_left)
    def _():
        tell_ring(across, left)

    @pl.when(at_border & at_right)
    def _():
        tell_ring(across, right)

    load_low.wait()
    mine = low[...].astype(F32)
    edge[0] = low[:, 0, :]
    edge[1] = low[:, 15, :]
    ext[1:5, 1:17] = mine
    ext[1:5, 0:1] = mine[:, 0:1]
    ext[1:5, 17:18] = mine[:, 15:16]
    ext[0] = ext[1]
    ext[5] = ext[4]
    for j in range(8):
        extw[:, j] = ext[:, 2 * j : 2 * j + 4].astype(BF16)
    pl.semaphore_wait(bar, FRAMES - 1 + 18)

    def window(to):
        r, j = patch_of(to, band)
        pltpu.make_async_remote_copy(
            src_ref=extw.at[pl.ds(r, 3), j], dst_ref=got.at[me],
            send_sem=in_send, recv_sem=in_recv,
            device_id=(base + to, col), device_id_type=MESH,
        ).start()

    def rim(src, kind, to, column):
        pltpu.make_async_remote_copy(
            src_ref=src, dst_ref=halo.at[kind, me], send_sem=h_send, recv_sem=h_recv.at[kind],
            device_id=(to, column), device_id_type=MESH,
        ).start()

    def rims():
        for to in (0, 8, 10, 12):
            rim(edge.at[1], 0, base + to, right)
        for to in (7, 9, 11, 13):
            rim(edge.at[0], 1, base + to, left)
        for to in range(8):
            rim(extw.at[border + 1, to], 2, across + to, col)
        rim(edge.at[1], 3, across, right)
        rim(edge.at[0], 4, across + 7, left)

    early = me < EARLY

    @pl.when(early)
    def _():
        for s in ACROSS_OFFSETS:
            window(EARLY + (me + s) % EARLY)
        rims()
        for s in GROUP_OFFSETS:
            window((me + s) % EARLY)

    @pl.when(jnp.logical_not(early))
    def _():
        for s in GROUP_OFFSETS:
            window(EARLY + (me + s) % EARLY)
        rims()
        for s in ACROSS_OFFSETS:
            window((me + s) % EARLY)

    got[me] = extw[pl.ds(patch_row, 3), patch_col]

    pltpu.make_async_copy(got.at[pl.ds(0, 31)], got.at[pl.ds(0, 31)], in_recv).wait()
    for f in range(FRAMES):
        for k in range(3):
            gf[12 * f + 4 * k : 12 * f + 4 * k + 4] = got[f, k].astype(F32)

    def take(kind):
        pltpu.make_async_copy(halo.at[kind], halo.at[kind], h_recv.at[kind]).wait()
        for f in range(FRAMES):
            gh[4 * f : 4 * f + 4] = halo[kind, f].astype(F32)

    border_row = jnp.where(band == 0, 2, 0)
    other_row = jnp.where(band == 0, 0, 3)

    @pl.when(at_border)
    def _():
        take(2)
        for c in range(4):
            gf[pl.ds(4 * border_row + c, FRAMES, stride=12)] = gh[pl.ds(c, FRAMES, stride=4)]

    def side(kind, c, inside):
        take(kind)

        @pl.when(inside)
        def _():
            for k in range(3):
                r = jnp.clip(patch_row - 1 + k, 0, 3)
                gf[pl.ds(4 * k + c, FRAMES, stride=12)] = gh[pl.ds(r, FRAMES, stride=4)]

        @pl.when(at_border)
        def _():
            take(kind + 3)

            @pl.when(inside)
            def _():
                gf[pl.ds(4 * border_row + c, FRAMES, stride=12)] = gh[
                    pl.ds(other_row, FRAMES, stride=4)
                ]

    @pl.when(at_left)
    def _():
        side(0, 0, col > 0)

    @pl.when(at_right)
    def _():
        side(1, 3, col < 7)

    grid = [[gf[pl.ds(4 * k + c, FRAMES, stride=12)] for c in range(4)] for k in range(3)]
    columns = [spread([grid[k][c] for k in range(3)]) for c in range(4)]
    keep_top = jnp.where((band == 0) & (patch_row == 0), 0.0, 1.0).astype(F32)
    keep_bottom = jnp.where((band == 1) & (patch_row == 3), 0.0, 1.0).astype(F32)
    keep_left = jnp.where((col == 0) & at_left, 0.0, 1.0).astype(F32)
    keep_right = jnp.where((col == 7) & at_right, 0.0, 1.0).astype(F32)
    for y in range(6):
        row = spread([columns[c][y] for c in range(4)])
        for x in range(10):
            value = row[x]
            if y == 0:
                value = value * keep_top
            if y == 5:
                value = value * keep_bottom
            if x == 0:
                value = value * keep_left
            if x == 9:
                value = value * keep_right
            u[y, x] = value.astype(BF16)

    load_w.wait()
    load_ain.wait()
    load_aout.wait()

    lane = lax.broadcasted_iota(jnp.int32, (128, CH), 1)
    head0 = (lane < 64).astype(F32).astype(BF16)
    head1 = (lane >= 64).astype(F32).astype(BF16)
    ones = jnp.concatenate([head0, head1], axis=0)
    s_row = lax.broadcasted_iota(jnp.int32, (128, 256), 0) // FRAMES
    s_lane = lax.broadcasted_iota(jnp.int32, (128, 256), 1) % 128 // FRAMES
    same_pixel = s_row == s_lane

    def give(h, frame):
        top, bottom = PIECES[h]

        @pl.when(frame != me)
        def _():
            pltpu.make_async_remote_copy(
                src_ref=snd.at[frame, top:bottom], dst_ref=out.at[patch, top:bottom],
                send_sem=o_send.at[h], recv_sem=o_recv.at[h],
                device_id=(base + frame, col), device_id_type=MESH,
            ).start()

    for h, (top, bottom) in enumerate(PIECES):
        pixels = 8 * (bottom - top)
        rows = pixels * FRAMES
        frame_id = lax.broadcasted_iota(jnp.int32, (rows, CH), 0) % FRAMES
        lhs = jnp.concatenate(
            [
                u[top + dy : bottom + dy, dx : dx + 8].reshape(rows, CH)
                for dy in range(3)
                for dx in range(3)
            ],
            axis=1,
        )
        w01 = jnp.concatenate([w[0:1152], w[1152:2304]], axis=1)
        y01 = jnp.dot(lhs, w01, preferred_element_type=F32)
        y2 = jnp.dot(lhs, w[2304:3456], preferred_element_type=F32)
        before = jnp.where(frame_id == 0, 0.0, pltpu.roll(y01[:, :CH], 1, 0))
        after = jnp.where(frame_id == FRAMES - 1, 0.0, pltpu.roll(y2, rows - 1, 0))
        total = before + y01[:, CH:] + after
        centre = u[top + 1 : bottom + 1, 1:9].reshape(rows, CH).astype(F32)
        feat = (centre + total / (1.0 + jnp.exp(-total))).astype(BF16)
        proj = jnp.dot(feat, ain[...], preferred_element_type=F32).astype(BF16)
        for g in range(rows // 128):
            part = proj[128 * g : 128 * g + 128]
            q = part[:, :CH]
            k = part[:, CH : 2 * CH]
            v = part[:, 2 * CH :]
            keys = jnp.concatenate([k * head0, k * head1], axis=0)
            scores = lax.dot_general(
                q, keys, (((1,), (1,)), ((), ())), preferred_element_type=F32
            )
            scores = jnp.where(same_pixel, scores * 0.125, -1e30)
            m0 = jnp.max(scores[:, :128], axis=1, keepdims=True)
            m1 = jnp.max(scores[:, 128:], axis=1, keepdims=True)
            expo = jnp.concatenate(
                [jnp.exp(scores[:, :128] - m0), jnp.exp(scores[:, 128:] - m1)], axis=1
            ).astype(BF16)
            values = jnp.concatenate([v * head0, v * head1], axis=0)
            summed = jnp.dot(
                expo, jnp.concatenate([values, ones], axis=1), preferred_element_type=F32
            )
            context = (summed[:, :CH] / summed[:, CH:]).astype(BF16)
            output = jnp.dot(context, aout[...], preferred_element_type=F32)
            rf[128 * g : 128 * g + 128] = feat[128 * g : 128 * g + 128].astype(F32) + output
        for f in range(FRAMES):
            for y in range(bottom - top):
                snd[f, top + y] = rf[pl.ds(256 * y + f, 8, stride=FRAMES)].astype(BF16)
        for lo in (0, EARLY):
            for s in range(EARLY):
                give(h, lo + (me + s) % EARLY)
        out[patch, top:bottom] = snd[me, top:bottom]

    sent = halo.at[0, pl.ds(0, 18)]
    pltpu.make_async_copy(sent, sent, h_send).wait()
    pltpu.make_async_copy(got.at[pl.ds(0, 31)], got.at[pl.ds(0, 31)], in_send).wait()
    for h, (top, bottom) in enumerate(PIECES):
        block = snd.at[pl.ds(0, 31), top:bottom]
        pltpu.make_async_copy(block, block, o_send.at[h]).wait()
        pltpu.make_async_copy(block, block, o_recv.at[h]).wait()


def local(low_frames, conv_weight, attn_in, attn_out):
    vmem = pltpu.VMEM
    dma = pltpu.SemaphoreType.DMA
    patches = pl.pallas_call(
        kernel,
        out_shape=jax.ShapeDtypeStruct((FRAMES, 4, 8, CH), BF16),
        in_specs=[pl.BlockSpec(memory_space=pl.ANY)] * 4,
        out_specs=pl.BlockSpec(memory_space=pltpu.VMEM),
        scratch_shapes=[
            vmem((4, 16, CH), BF16),
            vmem((27 * CH, CH), BF16),
            vmem((CH, 3 * CH), BF16),
            vmem((CH, CH), BF16),
            vmem((2, 4, CH), BF16),
            vmem((6, 24, CH), F32),
            vmem((6, 8, 4, CH), BF16),
            vmem((FRAMES, 3, 4, CH), BF16),
            vmem((5, FRAMES, 4, CH), BF16),
            vmem((FRAMES * 12, CH), F32),
            vmem((FRAMES * 4, CH), F32),
            vmem((6, 10, FRAMES, CH), BF16),
            vmem((32 * FRAMES, CH), F32),
            vmem((FRAMES, 4, 8, CH), BF16),
            dma((4,)),
            dma,
            dma,
            dma,
            dma((5,)),
            dma((len(PIECES),)),
            dma((len(PIECES),)),
        ],
        compiler_params=pltpu.CompilerParams(
            collective_id=0, has_side_effects=True, vmem_limit_bytes=56 * 1024 * 1024
        ),
    )(low_frames, conv_weight, attn_in, attn_out)
    blocks = patches.reshape(4, 8, 4, 8, CH)
    return jnp.transpose(blocks, (0, 2, 1, 3, 4)).reshape(16, 64, CH)


def solution(mesh):
    in_specs = (P("rows", "cols", None), P(), P(), P())
    out_specs = P("rows", "cols", None)
    return jax.shard_map(local, mesh=mesh, in_specs=in_specs, out_specs=out_specs, check_vma=False)
```

```python
import jax
import jax.numpy as jnp
from jax import lax
from jax.experimental import pallas as pl
from jax.experimental.pallas import tpu as pltpu
from jax.sharding import PartitionSpec as P

MESH = pl.DeviceIdType.MESH
F32 = jnp.float32
BF16 = jnp.bfloat16
FRAMES = 32
EARLY = 16
GROUP_OFFSETS = [s for d in range(8, 0, -1) for s in ((d,) if d == 8 else (d, 16 - d))]
ACROSS_OFFSETS = [0] + GROUP_OFFSETS[::-1]
CH = 128
PARTS = ((0, 2), (2, 3))
PIECES = ((0, 1), (1, 4))
OFFSETS = [s for d in range(16, 0, -1) for s in ((d,) if d == 16 else (d, 32 - d))]
TAPS = ((0.375, 0.625), (0.125, 0.875), (0.875, 0.125), (0.625, 0.375))


def lerp(weights, a, b):
    return weights[0] * a + weights[1] * b


def spread(x):
    out = [lerp(TAPS[3], x[0], x[1])]
    for k in range(1, len(x) - 1):
        out.append(lerp(TAPS[0], x[k - 1], x[k]))
        out.append(lerp(TAPS[1], x[k - 1], x[k]))
        out.append(lerp(TAPS[2], x[k], x[k + 1]))
        out.append(lerp(TAPS[3], x[k], x[k + 1]))
    out.append(lerp(TAPS[0], x[-2], x[-1]))
    return out


def patch_of(index, band):
    rest = index - 14
    depth = jnp.where(
        index < 8, 0, jnp.where(index < 14, 1 + (index - 8) // 2, 1 + rest // 6)
    )
    column = jnp.where(
        index < 8, index, jnp.where(index < 14, 7 * (index % 2), 1 + rest % 6)
    )
    return jnp.where(band == 0, 3 - depth, depth), column


def kernel(
    low_hbm, w_hbm, ain_hbm, aout_hbm, out,
    low, w, ain, aout, edge, ext, extw, got, halo, gf, gh, u, rf, snd,
    ld_sem, in_send, in_recv, h_send, h_recv, o_send, o_recv,
):
    place = lax.axis_index("rows")
    col = lax.axis_index("cols")
    band = place // FRAMES
    me = place % FRAMES
    base = band * FRAMES
    across = (1 - band) * FRAMES
    left = (col + 7) % 8
    right = (col + 1) % 8
    patch_row, patch_col = patch_of(me, band)
    patch = patch_row * 8 + patch_col
    border = jnp.where(band == 0, 3, 0)
    at_border = patch_row == border
    at_left = patch_col == 0
    at_right = patch_col == 7

    def load(k, src, dst):
        cp = pltpu.make_async_copy(src, dst, ld_sem.at[k])
        cp.start()
        return cp

    load_low = load(0, low_hbm, low)
    load_w = load(1, w_hbm, w)
    load_ain = load(2, ain_hbm, ain)
    load_aout = load(3, aout_hbm, aout)

    bar = pltpu.get_barrier_semaphore()

    def tell(row, column):
        pl.semaphore_signal(bar, inc=1, device_id=(row, column), device_id_type=MESH)

    def tell_ring(ring, column):
        def one(f, _):
            tell(ring + f, column)
            return _

        lax.fori_loop(0, FRAMES, one, 0)

    for s in OFFSETS:
        tell(base + (me + s) % FRAMES, col)

    @pl.when(at_left)
    def _():
        tell_ring(base, left)

    @pl.when(at_right)
    def _():
        tell_ring(base, right)

    @pl.when(at_border)
    def _():
        tell_ring(across, col)

    @pl.when(at_border & at_left)
    def _():
        tell_ring(across, left)

    @pl.when(at_border & at_right)
    def _():
        tell_ring(across, right)

    load_low.wait()
    mine = low[...].astype(F32)
    edge[0] = low[:, 0, :]
    edge[1] = low[:, 15, :]
    ext[1:5, 1:17] = mine
    ext[1:5, 0:1] = mine[:, 0:1]
    ext[1:5, 17:18] = mine[:, 15:16]
    ext[0] = ext[1]
    ext[5] = ext[4]
    for j in range(8):
        extw[:, j] = ext[:, 2 * j : 2 * j + 4].astype(BF16)
    pl.semaphore_wait(bar, FRAMES - 1 + 18)

    def window(to, part):
        lo, hi = PARTS[part]
        r, j = patch_of(to, band)
        pltpu.make_async_remote_copy(
            src_ref=extw.at[pl.ds(r + lo, hi - lo), j], dst_ref=got.at[me, lo:hi],
            send_sem=in_send, recv_sem=in_recv.at[part],
            device_id=(base + to, col), device_id_type=MESH,
        ).start()

    def rim(src, kind, to, column):
        pltpu.make_async_remote_copy(
            src_ref=src, dst_ref=halo.at[kind, me], send_sem=h_send, recv_sem=h_recv.at[kind],
            device_id=(to, column), device_id_type=MESH,
        ).start()

    def rims():
        for to in (0, 8, 10, 12):
            rim(edge.at[1], 0, base + to, right)
        for to in (7, 9, 11, 13):
            rim(edge.at[0], 1, base + to, left)
        for to in range(8):
            rim(extw.at[border + 1, to], 2, across + to, col)
        rim(edge.at[1], 3, across, right)
        rim(edge.at[0], 4, across + 7, left)

    early = me < EARLY

    @pl.when(early)
    def _():
        for part in range(2):
            for s in ACROSS_OFFSETS:
                window(EARLY + (me + s) % EARLY, part)
            if part == 0:
                rims()
            for s in GROUP_OFFSETS:
                window((me + s) % EARLY, part)

    @pl.when(jnp.logical_not(early))
    def _():
        for part in range(2):
            for s in GROUP_OFFSETS:
                window(EARLY + (me + s) % EARLY, part)
            if part == 0:
                rims()
            for s in ACROSS_OFFSETS:
                window((me + s) % EARLY, part)

    got[me] = extw[pl.ds(patch_row, 3), patch_col]

    border_row = jnp.where(band == 0, 2, 0)
    other_row = jnp.where(band == 0, 0, 3)
    sides = ((0, 0, at_left, col > 0), (1, 3, at_right, col < 7))

    def take(kind, wanted):
        @pl.when(wanted)
        def _():
            pltpu.make_async_copy(halo.at[kind], halo.at[kind], h_recv.at[kind]).wait()
            for f in range(FRAMES):
                gh[kind, 4 * f : 4 * f + 4] = halo[kind, f].astype(F32)

    def arrive(part):
        lo, hi = PARTS[part]
        block = got.at[pl.ds(0, 31), lo:hi]
        pltpu.make_async_copy(block, block, in_recv.at[part]).wait()
        for f in range(FRAMES):
            for k in range(lo, hi):
                gf[12 * f + 4 * k : 12 * f + 4 * k + 4] = got[f, k].astype(F32)
        has_border = at_border & (band == 1 - part)

        @pl.when(has_border)
        def _():
            for c in range(4):
                gf[pl.ds(4 * border_row + c, FRAMES, stride=12)] = gh[
                    2, pl.ds(c, FRAMES, stride=4)
                ]

        for kind, c, at_side, inside in sides:

            @pl.when(at_side & inside)
            def _():
                for k in range(lo, hi):
                    r = jnp.clip(patch_row - 1 + k, 0, 3)
                    gf[pl.ds(4 * k + c, FRAMES, stride=12)] = gh[
                        kind, pl.ds(r, FRAMES, stride=4)
                    ]

            @pl.when(at_side & inside & has_border)
            def _():
                gf[pl.ds(4 * border_row + c, FRAMES, stride=12)] = gh[
                    kind + 3, pl.ds(other_row, FRAMES, stride=4)
                ]

    keep_top = jnp.where((band == 0) & (patch_row == 0), 0.0, 1.0).astype(F32)
    keep_bottom = jnp.where((band == 1) & (patch_row == 3), 0.0, 1.0).astype(F32)
    keep_left = jnp.where((col == 0) & at_left, 0.0, 1.0).astype(F32)
    keep_right = jnp.where((col == 7) & at_right, 0.0, 1.0).astype(F32)
    def lift(k, lines):
        two = [[gf[pl.ds(4 * i + c, FRAMES, stride=12)] for c in range(4)] for i in (k, k + 1)]
        for y, taps in lines:
            row = spread([lerp(taps, two[0][c], two[1][c]) for c in range(4)])
            for x in range(10):
                value = row[x]
                if y == 0:
                    value = value * keep_top
                if y == 5:
                    value = value * keep_bottom
                if x == 0:
                    value = value * keep_left
                if x == 9:
                    value = value * keep_right
                u[y, x] = value.astype(BF16)

    take(0, at_left)
    take(1, at_right)
    take(2, at_border)
    take(3, at_border & at_left)
    take(4, at_border & at_right)
    arrive(0)
    lift(0, ((0, TAPS[3]), (1, TAPS[0]), (2, TAPS[1])))

    load_w.wait()
    load_ain.wait()
    load_aout.wait()

    lane = lax.broadcasted_iota(jnp.int32, (128, CH), 1)
    head0 = (lane < 64).astype(F32).astype(BF16)
    head1 = (lane >= 64).astype(F32).astype(BF16)
    ones = jnp.concatenate([head0, head1], axis=0)
    s_row = lax.broadcasted_iota(jnp.int32, (128, 256), 0) // FRAMES
    s_lane = lax.broadcasted_iota(jnp.int32, (128, 256), 1) % 128 // FRAMES
    same_pixel = s_row == s_lane

    def give(h, frame):
        top, bottom = PIECES[h]

        @pl.when(frame != me)
        def _():
            pltpu.make_async_remote_copy(
                src_ref=snd.at[frame, top:bottom], dst_ref=out.at[patch, top:bottom],
                send_sem=o_send.at[h], recv_sem=o_recv.at[h],
                device_id=(base + frame, col), device_id_type=MESH,
            ).start()

    own = []
    for h, (top, bottom) in enumerate(PIECES):
        if h == 1:
            arrive(1)
            lift(1, ((3, TAPS[2]), (4, TAPS[3]), (5, TAPS[0])))
        pixels = 8 * (bottom - top)
        rows = pixels * FRAMES
        frame_id = lax.broadcasted_iota(jnp.int32, (rows, CH), 0) % FRAMES
        lhs = jnp.concatenate(
            [
                u[top + dy : bottom + dy, dx : dx + 8].reshape(rows, CH)
                for dy in range(3)
                for dx in range(3)
            ],
            axis=1,
        )
        w01 = jnp.concatenate([w[0:1152], w[1152:2304]], axis=1)
        y01 = jnp.dot(lhs, w01, preferred_element_type=F32)
        y2 = jnp.dot(lhs, w[2304:3456], preferred_element_type=F32)
        before = jnp.where(frame_id == 0, 0.0, pltpu.roll(y01[:, :CH], 1, 0))
        after = jnp.where(frame_id == FRAMES - 1, 0.0, pltpu.roll(y2, rows - 1, 0))
        total = before + y01[:, CH:] + after
        centre = u[top + 1 : bottom + 1, 1:9].reshape(rows, CH).astype(F32)
        feat = (centre + total / (1.0 + jnp.exp(-total))).astype(BF16)
        proj = jnp.dot(feat, ain[...], preferred_element_type=F32).astype(BF16)
        for g in range(rows // 128):
            part = proj[128 * g : 128 * g + 128]
            q = part[:, :CH]
            k = part[:, CH : 2 * CH]
            v = part[:, 2 * CH :]
            keys = jnp.concatenate([k * head0, k * head1], axis=0)
            scores = lax.dot_general(
                q, keys, (((1,), (1,)), ((), ())), preferred_element_type=F32
            )
            scores = jnp.where(same_pixel, scores * 0.125, -1e30)
            m0 = jnp.max(scores[:, :128], axis=1, keepdims=True)
            m1 = jnp.max(scores[:, 128:], axis=1, keepdims=True)
            expo = jnp.concatenate(
                [jnp.exp(scores[:, :128] - m0), jnp.exp(scores[:, 128:] - m1)], axis=1
            ).astype(BF16)
            values = jnp.concatenate([v * head0, v * head1], axis=0)
            summed = jnp.dot(
                expo, jnp.concatenate([values, ones], axis=1), preferred_element_type=F32
            )
            context = (summed[:, :CH] / summed[:, CH:]).astype(BF16)
            output = jnp.dot(context, aout[...], preferred_element_type=F32)
            rf[128 * g : 128 * g + 128] = feat[128 * g : 128 * g + 128].astype(F32) + output
        for f in range(FRAMES):
            for y in range(bottom - top):
                snd[f, top + y] = rf[pl.ds(256 * y + f, 8, stride=FRAMES)].astype(BF16)
        for lo in (0, EARLY):
            for s in range(EARLY):
                give(h, lo + (me + s) % EARLY)
        own.append(load(4 + h, snd.at[me, top:bottom], out.at[patch, top:bottom]))

    sent = halo.at[0, pl.ds(0, 18)]
    pltpu.make_async_copy(sent, sent, h_send).wait()
    pltpu.make_async_copy(got.at[pl.ds(0, 31)], got.at[pl.ds(0, 31)], in_send).wait()
    for h, (top, bottom) in enumerate(PIECES):
        block = snd.at[pl.ds(0, 31), top:bottom]
        pltpu.make_async_copy(block, block, o_send.at[h]).wait()
        pltpu.make_async_copy(block, block, o_recv.at[h]).wait()
        own[h].wait()


def local(low_frames, conv_weight, attn_in, attn_out):
    vmem = pltpu.VMEM
    dma = pltpu.SemaphoreType.DMA
    patches = pl.pallas_call(
        kernel,
        out_shape=jax.ShapeDtypeStruct((FRAMES, 4, 8, CH), BF16),
        in_specs=[pl.BlockSpec(memory_space=pl.ANY)] * 4,
        out_specs=pl.BlockSpec(memory_space=pl.ANY),
        scratch_shapes=[
            vmem((4, 16, CH), BF16),
            vmem((27 * CH, CH), BF16),
            vmem((CH, 3 * CH), BF16),
            vmem((CH, CH), BF16),
            vmem((2, 4, CH), BF16),
            vmem((6, 24, CH), F32),
            vmem((6, 8, 4, CH), BF16),
            vmem((FRAMES, 3, 4, CH), BF16),
            vmem((5, FRAMES, 4, CH), BF16),
            vmem((FRAMES * 12, CH), F32),
            vmem((5, FRAMES * 4, CH), F32),
            vmem((6, 10, FRAMES, CH), BF16),
            vmem((32 * FRAMES, CH), F32),
            vmem((FRAMES, 4, 8, CH), BF16),
            dma((4 + len(PIECES),)),
            dma,
            dma((2,)),
            dma,
            dma((5,)),
            dma((len(PIECES),)),
            dma((len(PIECES),)),
        ],
        compiler_params=pltpu.CompilerParams(
            collective_id=0, has_side_effects=True, vmem_limit_bytes=56 * 1024 * 1024
        ),
    )(low_frames, conv_weight, attn_in, attn_out)
    blocks = patches.reshape(4, 8, 4, 8, CH)
    return jnp.transpose(blocks, (0, 2, 1, 3, 4)).reshape(16, 64, CH)


def solution(mesh):
    in_specs = (P("rows", "cols", None), P(), P(), P())
    out_specs = P("rows", "cols", None)
    return jax.shard_map(local, mesh=mesh, in_specs=in_specs, out_specs=out_specs, check_vma=False)
```

```python
import jax
import jax.numpy as jnp
from jax import lax
from jax.experimental import pallas as pl
from jax.experimental.pallas import tpu as pltpu
from jax.sharding import PartitionSpec as P

MESH = pl.DeviceIdType.MESH
F32 = jnp.float32
BF16 = jnp.bfloat16
FRAMES = 32
EARLY = 16
GROUP_OFFSETS = [s for d in range(8, 0, -1) for s in ((d,) if d == 8 else (d, 16 - d))]
ACROSS_OFFSETS = [0] + GROUP_OFFSETS[::-1]
CH = 128
PARTS = ((0, 2), (2, 3))
PIECES = ((0, 1), (1, 4))
OFFSETS = [s for d in range(16, 0, -1) for s in ((d,) if d == 16 else (d, 32 - d))]
TAPS = ((0.375, 0.625), (0.125, 0.875), (0.875, 0.125), (0.625, 0.375))


def lerp(weights, a, b):
    return weights[0] * a + weights[1] * b


def spread(x):
    out = [lerp(TAPS[3], x[0], x[1])]
    for k in range(1, len(x) - 1):
        out.append(lerp(TAPS[0], x[k - 1], x[k]))
        out.append(lerp(TAPS[1], x[k - 1], x[k]))
        out.append(lerp(TAPS[2], x[k], x[k + 1]))
        out.append(lerp(TAPS[3], x[k], x[k + 1]))
    out.append(lerp(TAPS[0], x[-2], x[-1]))
    return out


def patch_of(index, band):
    rest = index - 14
    depth = jnp.where(
        index < 8, 0, jnp.where(index < 14, 1 + (index - 8) // 2, 1 + rest // 6)
    )
    column = jnp.where(
        index < 8, index, jnp.where(index < 14, 7 * (index % 2), 1 + rest % 6)
    )
    return jnp.where(band == 0, 3 - depth, depth), column


def kernel(
    low_hbm, w_hbm, ain_hbm, aout_hbm, out,
    low, w, ain, aout, edge, ext, extw, got, halo, gf, gh, u, rf, snd,
    ld_sem, in_send, in_recv, h_send, h_recv, o_send, o_recv,
):
    place = lax.axis_index("rows")
    col = lax.axis_index("cols")
    band = place // FRAMES
    me = place % FRAMES
    base = band * FRAMES
    across = (1 - band) * FRAMES
    left = (col + 7) % 8
    right = (col + 1) % 8
    patch_row, patch_col = patch_of(me, band)
    patch = patch_row * 8 + patch_col
    border = jnp.where(band == 0, 3, 0)
    at_border = patch_row == border
    at_left = patch_col == 0
    at_right = patch_col == 7

    def load(k, src, dst):
        cp = pltpu.make_async_copy(src, dst, ld_sem.at[k])
        cp.start()
        return cp

    load_low = load(0, low_hbm, low)
    load_w = load(1, w_hbm, w)
    load_ain = load(2, ain_hbm, ain)
    load_aout = load(3, aout_hbm, aout)

    bar = pltpu.get_barrier_semaphore()

    def tell(row, column):
        pl.semaphore_signal(bar, inc=1, device_id=(row, column), device_id_type=MESH)

    def tell_ring(ring, column):
        def one(f, _):
            tell(ring + f, column)
            return _

        lax.fori_loop(0, FRAMES, one, 0)

    for s in OFFSETS:
        tell(base + (me + s) % FRAMES, col)

    @pl.when(at_left)
    def _():
        tell_ring(base, left)

    @pl.when(at_right)
    def _():
        tell_ring(base, right)

    @pl.when(at_border)
    def _():
        tell_ring(across, col)

    @pl.when(at_border & at_left)
    def _():
        tell_ring(across, left)

    @pl.when(at_border & at_right)
    def _():
        tell_ring(across, right)

    load_low.wait()
    mine = low[...].astype(F32)
    edge[0] = low[:, 0, :]
    edge[1] = low[:, 15, :]
    ext[1:5, 1:17] = mine
    ext[1:5, 0:1] = mine[:, 0:1]
    ext[1:5, 17:18] = mine[:, 15:16]
    ext[0] = ext[1]
    ext[5] = ext[4]
    for j in range(8):
        extw[:, j] = ext[:, 2 * j : 2 * j + 4].astype(BF16)
    pl.semaphore_wait(bar, FRAMES - 1 + 18)

    def window(to, part):
        lo, hi = PARTS[part]
        r, j = patch_of(to, band)
        pltpu.make_async_remote_copy(
            src_ref=extw.at[pl.ds(r + lo, hi - lo), j], dst_ref=got.at[me, lo:hi],
            send_sem=in_send, recv_sem=in_recv.at[part],
            device_id=(base + to, col), device_id_type=MESH,
        ).start()

    def rim(src, kind, to, column):
        pltpu.make_async_remote_copy(
            src_ref=src, dst_ref=halo.at[kind, me], send_sem=h_send, recv_sem=h_recv.at[kind],
            device_id=(to, column), device_id_type=MESH,
        ).start()

    def rims():
        for to in (0, 8, 10, 12):
            rim(edge.at[1], 0, base + to, right)
        for to in (7, 9, 11, 13):
            rim(edge.at[0], 1, base + to, left)
        for to in range(8):
            rim(extw.at[border + 1, to], 2, across + to, col)
        rim(edge.at[1], 3, across, right)
        rim(edge.at[0], 4, across + 7, left)

    early = me < EARLY

    @pl.when(early)
    def _():
        for part in range(2):
            if part == 0:
                rims()
            for s in ACROSS_OFFSETS:
                window(EARLY + (me + s) % EARLY, part)
            for s in GROUP_OFFSETS:
                window((me + s) % EARLY, part)

    @pl.when(jnp.logical_not(early))
    def _():
        for part in range(2):
            for s in GROUP_OFFSETS:
                window(EARLY + (me + s) % EARLY, part)
            if part == 0:
                rims()
            for s in ACROSS_OFFSETS:
                window((me + s) % EARLY, part)

    got[me] = extw[pl.ds(patch_row, 3), patch_col]

    border_row = jnp.where(band == 0, 2, 0)
    other_row = jnp.where(band == 0, 0, 3)
    sides = ((0, 0, at_left, col > 0), (1, 3, at_right, col < 7))

    def take(kind, wanted):
        @pl.when(wanted)
        def _():
            pltpu.make_async_copy(halo.at[kind], halo.at[kind], h_recv.at[kind]).wait()
            for f in range(FRAMES):
                gh[kind, 4 * f : 4 * f + 4] = halo[kind, f].astype(F32)

    def arrive(part):
        lo, hi = PARTS[part]
        block = got.at[pl.ds(0, 31), lo:hi]
        pltpu.make_async_copy(block, block, in_recv.at[part]).wait()
        for f in range(FRAMES):
            for k in range(lo, hi):
                gf[12 * f + 4 * k : 12 * f + 4 * k + 4] = got[f, k].astype(F32)
        has_border = at_border & (band == 1 - part)

        @pl.when(has_border)
        def _():
            for c in range(4):
                gf[pl.ds(4 * border_row + c, FRAMES, stride=12)] = gh[
                    2, pl.ds(c, FRAMES, stride=4)
                ]

        for kind, c, at_side, inside in sides:

            @pl.when(at_side & inside)
            def _():
                for k in range(lo, hi):
                    r = jnp.clip(patch_row - 1 + k, 0, 3)
                    gf[pl.ds(4 * k + c, FRAMES, stride=12)] = gh[
                        kind, pl.ds(r, FRAMES, stride=4)
                    ]

            @pl.when(at_side & inside & has_border)
            def _():
                gf[pl.ds(4 * border_row + c, FRAMES, stride=12)] = gh[
                    kind + 3, pl.ds(other_row, FRAMES, stride=4)
                ]

    keep_top = jnp.where((band == 0) & (patch_row == 0), 0.0, 1.0).astype(F32)
    keep_bottom = jnp.where((band == 1) & (patch_row == 3), 0.0, 1.0).astype(F32)
    keep_left = jnp.where((col == 0) & at_left, 0.0, 1.0).astype(F32)
    keep_right = jnp.where((col == 7) & at_right, 0.0, 1.0).astype(F32)
    def lift(k, lines):
        two = [[gf[pl.ds(4 * i + c, FRAMES, stride=12)] for c in range(4)] for i in (k, k + 1)]
        for y, taps in lines:
            row = spread([lerp(taps, two[0][c], two[1][c]) for c in range(4)])
            for x in range(10):
                value = row[x]
                if y == 0:
                    value = value * keep_top
                if y == 5:
                    value = value * keep_bottom
                if x == 0:
                    value = value * keep_left
                if x == 9:
                    value = value * keep_right
                u[y, x] = value.astype(BF16)

    take(0, at_left)
    take(1, at_right)
    take(2, at_border)
    take(3, at_border & at_left)
    take(4, at_border & at_right)
    arrive(0)
    lift(0, ((0, TAPS[3]), (1, TAPS[0]), (2, TAPS[1])))

    load_w.wait()
    load_ain.wait()
    load_aout.wait()

    lane = lax.broadcasted_iota(jnp.int32, (128, CH), 1)
    head0 = (lane < 64).astype(F32).astype(BF16)
    head1 = (lane >= 64).astype(F32).astype(BF16)
    ones = jnp.concatenate([head0, head1], axis=0)
    s_row = lax.broadcasted_iota(jnp.int32, (128, 256), 0) // FRAMES
    s_lane = lax.broadcasted_iota(jnp.int32, (128, 256), 1) % 128 // FRAMES
    same_pixel = s_row == s_lane

    def give(h, frame):
        top, bottom = PIECES[h]

        @pl.when(frame != me)
        def _():
            pltpu.make_async_remote_copy(
                src_ref=snd.at[frame, top:bottom], dst_ref=out.at[patch, top:bottom],
                send_sem=o_send.at[h], recv_sem=o_recv.at[h],
                device_id=(base + frame, col), device_id_type=MESH,
            ).start()

    own = []
    for h, (top, bottom) in enumerate(PIECES):
        if h == 1:
            arrive(1)
            lift(1, ((3, TAPS[2]), (4, TAPS[3]), (5, TAPS[0])))
        pixels = 8 * (bottom - top)
        rows = pixels * FRAMES
        frame_id = lax.broadcasted_iota(jnp.int32, (rows, CH), 0) % FRAMES
        lhs = jnp.concatenate(
            [
                u[top + dy : bottom + dy, dx : dx + 8].reshape(rows, CH)
                for dy in range(3)
                for dx in range(3)
            ],
            axis=1,
        )
        w01 = jnp.concatenate([w[0:1152], w[1152:2304]], axis=1)
        y01 = jnp.dot(lhs, w01, preferred_element_type=F32)
        y2 = jnp.dot(lhs, w[2304:3456], preferred_element_type=F32)
        before = jnp.where(frame_id == 0, 0.0, pltpu.roll(y01[:, :CH], 1, 0))
        after = jnp.where(frame_id == FRAMES - 1, 0.0, pltpu.roll(y2, rows - 1, 0))
        total = before + y01[:, CH:] + after
        centre = u[top + 1 : bottom + 1, 1:9].reshape(rows, CH).astype(F32)
        feat = (centre + total / (1.0 + jnp.exp(-total))).astype(BF16)
        proj = jnp.dot(feat, ain[...], preferred_element_type=F32).astype(BF16)
        for g in range(rows // 128):
            part = proj[128 * g : 128 * g + 128]
            q = part[:, :CH]
            k = part[:, CH : 2 * CH]
            v = part[:, 2 * CH :]
            keys = jnp.concatenate([k * head0, k * head1], axis=0)
            scores = lax.dot_general(
                q, keys, (((1,), (1,)), ((), ())), preferred_element_type=F32
            )
            scores = jnp.where(same_pixel, scores * 0.125, -1e30)
            m0 = jnp.max(scores[:, :128], axis=1, keepdims=True)
            m1 = jnp.max(scores[:, 128:], axis=1, keepdims=True)
            expo = jnp.concatenate(
                [jnp.exp(scores[:, :128] - m0), jnp.exp(scores[:, 128:] - m1)], axis=1
            ).astype(BF16)
            values = jnp.concatenate([v * head0, v * head1], axis=0)
            summed = jnp.dot(
                expo, jnp.concatenate([values, ones], axis=1), preferred_element_type=F32
            )
            context = (summed[:, :CH] / summed[:, CH:]).astype(BF16)
            output = jnp.dot(context, aout[...], preferred_element_type=F32)
            rf[128 * g : 128 * g + 128] = feat[128 * g : 128 * g + 128].astype(F32) + output
        for f in range(FRAMES):
            for y in range(bottom - top):
                snd[f, top + y] = rf[pl.ds(256 * y + f, 8, stride=FRAMES)].astype(BF16)
        for lo in (0, EARLY):
            for s in range(EARLY):
                give(h, lo + (me + s) % EARLY)
        own.append(load(4 + h, snd.at[me, top:bottom], out.at[patch, top:bottom]))

    sent = halo.at[0, pl.ds(0, 18)]
    pltpu.make_async_copy(sent, sent, h_send).wait()
    pltpu.make_async_copy(got.at[pl.ds(0, 31)], got.at[pl.ds(0, 31)], in_send).wait()
    for h, (top, bottom) in enumerate(PIECES):
        block = snd.at[pl.ds(0, 31), top:bottom]
        pltpu.make_async_copy(block, block, o_send.at[h]).wait()
        pltpu.make_async_copy(block, block, o_recv.at[h]).wait()
        own[h].wait()


def local(low_frames, conv_weight, attn_in, attn_out):
    vmem = pltpu.VMEM
    dma = pltpu.SemaphoreType.DMA
    patches = pl.pallas_call(
        kernel,
        out_shape=jax.ShapeDtypeStruct((FRAMES, 4, 8, CH), BF16),
        in_specs=[pl.BlockSpec(memory_space=pl.ANY)] * 4,
        out_specs=pl.BlockSpec(memory_space=pl.ANY),
        scratch_shapes=[
            vmem((4, 16, CH), BF16),
            vmem((27 * CH, CH), BF16),
            vmem((CH, 3 * CH), BF16),
            vmem((CH, CH), BF16),
            vmem((2, 4, CH), BF16),
            vmem((6, 24, CH), F32),
            vmem((6, 8, 4, CH), BF16),
            vmem((FRAMES, 3, 4, CH), BF16),
            vmem((5, FRAMES, 4, CH), BF16),
            vmem((FRAMES * 12, CH), F32),
            vmem((5, FRAMES * 4, CH), F32),
            vmem((6, 10, FRAMES, CH), BF16),
            vmem((32 * FRAMES, CH), F32),
            vmem((FRAMES, 4, 8, CH), BF16),
            dma((4 + len(PIECES),)),
            dma,
            dma((2,)),
            dma,
            dma((5,)),
            dma((len(PIECES),)),
            dma((len(PIECES),)),
        ],
        compiler_params=pltpu.CompilerParams(
            collective_id=0, has_side_effects=True, vmem_limit_bytes=56 * 1024 * 1024
        ),
    )(low_frames, conv_weight, attn_in, attn_out)
    blocks = patches.reshape(4, 8, 4, 8, CH)
    return jnp.transpose(blocks, (0, 2, 1, 3, 4)).reshape(16, 64, CH)


def solution(mesh):
    in_specs = (P("rows", "cols", None), P(), P(), P())
    out_specs = P("rows", "cols", None)
    return jax.shard_map(local, mesh=mesh, in_specs=in_specs, out_specs=out_specs, check_vma=False)
```

```python
import jax
import jax.numpy as jnp
from jax import lax
from jax.experimental import pallas as pl
from jax.experimental.pallas import tpu as pltpu
from jax.sharding import PartitionSpec as P

MESH = pl.DeviceIdType.MESH
F32 = jnp.float32
BF16 = jnp.bfloat16
FRAMES = 32
EARLY = 16
GROUP_OFFSETS = [s for d in range(8, 0, -1) for s in ((d,) if d == 8 else (d, 16 - d))]
ACROSS_OFFSETS = [0] + GROUP_OFFSETS[::-1]
CH = 128
PARTS = ((0, 2), (2, 3))
PIECES = ((0, 1), (1, 4))
OFFSETS = [s for d in range(16, 0, -1) for s in ((d,) if d == 16 else (d, 32 - d))]
TAPS = ((0.375, 0.625), (0.125, 0.875), (0.875, 0.125), (0.625, 0.375))


def lerp(weights, a, b):
    return weights[0] * a + weights[1] * b


def spread(x):
    out = [lerp(TAPS[3], x[0], x[1])]
    for k in range(1, len(x) - 1):
        out.append(lerp(TAPS[0], x[k - 1], x[k]))
        out.append(lerp(TAPS[1], x[k - 1], x[k]))
        out.append(lerp(TAPS[2], x[k], x[k + 1]))
        out.append(lerp(TAPS[3], x[k], x[k + 1]))
    out.append(lerp(TAPS[0], x[-2], x[-1]))
    return out


def patch_of(index, band):
    rest = index - 14
    depth = jnp.where(
        index < 8, 0, jnp.where(index < 14, 1 + (index - 8) // 2, 1 + rest // 6)
    )
    column = jnp.where(
        index < 8, index, jnp.where(index < 14, 7 * (index % 2), 1 + rest % 6)
    )
    return jnp.where(band == 0, 3 - depth, depth), column


def kernel(
    low_hbm, w_hbm, ain_hbm, aout_hbm, out,
    low, w, ain, aout, edge, ext, extw, got, halo, gf, gh, u, rf, snd,
    ld_sem, in_send, in_recv, h_send, h_recv, o_send, o_recv,
):
    place = lax.axis_index("rows")
    col = lax.axis_index("cols")
    band = place // FRAMES
    me = place % FRAMES
    base = band * FRAMES
    across = (1 - band) * FRAMES
    left = (col + 7) % 8
    right = (col + 1) % 8
    patch_row, patch_col = patch_of(me, band)
    patch = patch_row * 8 + patch_col
    border = jnp.where(band == 0, 3, 0)
    at_border = patch_row == border
    at_left = patch_col == 0
    at_right = patch_col == 7

    def load(k, src, dst):
        cp = pltpu.make_async_copy(src, dst, ld_sem.at[k])
        cp.start()
        return cp

    load_low = load(0, low_hbm, low)
    load_w = load(1, w_hbm, w)
    load_ain = load(2, ain_hbm, ain)
    load_aout = load(3, aout_hbm, aout)

    bar = pltpu.get_barrier_semaphore()

    def tell(row, column):
        pl.semaphore_signal(bar, inc=1, device_id=(row, column), device_id_type=MESH)

    def tell_ring(ring, column):
        def one(f, _):
            tell(ring + f, column)
            return _

        lax.fori_loop(0, FRAMES, one, 0)

    for s in OFFSETS:
        tell(base + (me + s) % FRAMES, col)

    @pl.when(at_left)
    def _():
        tell_ring(base, left)

    @pl.when(at_right)
    def _():
        tell_ring(base, right)

    @pl.when(at_border)
    def _():
        tell_ring(across, col)

    @pl.when(at_border & at_left)
    def _():
        tell_ring(across, left)

    @pl.when(at_border & at_right)
    def _():
        tell_ring(across, right)

    load_low.wait()
    mine = low[...].astype(F32)
    edge[0] = low[:, 0, :]
    edge[1] = low[:, 15, :]
    ext[1:5, 1:17] = mine
    ext[1:5, 0:1] = mine[:, 0:1]
    ext[1:5, 17:18] = mine[:, 15:16]
    ext[0] = ext[1]
    ext[5] = ext[4]
    for j in range(8):
        extw[:, j] = ext[:, 2 * j : 2 * j + 4].astype(BF16)
    pl.semaphore_wait(bar, FRAMES - 1 + 18)

    def window(to, part):
        lo, hi = PARTS[part]
        r, j = patch_of(to, band)
        pltpu.make_async_remote_copy(
            src_ref=extw.at[pl.ds(r + lo, hi - lo), j], dst_ref=got.at[me, lo:hi],
            send_sem=in_send, recv_sem=in_recv.at[part],
            device_id=(base + to, col), device_id_type=MESH,
        ).start()

    def rim(src, kind, to, column):
        pltpu.make_async_remote_copy(
            src_ref=src, dst_ref=halo.at[kind, me], send_sem=h_send, recv_sem=h_recv.at[kind],
            device_id=(to, column), device_id_type=MESH,
        ).start()

    def rims():
        for to in (0, 8, 10, 12):
            rim(edge.at[1], 0, base + to, right)
        for to in (7, 9, 11, 13):
            rim(edge.at[0], 1, base + to, left)
        for to in range(8):
            rim(extw.at[border + 1, to], 2, across + to, col)
        rim(edge.at[1], 3, across, right)
        rim(edge.at[0], 4, across + 7, left)

    early = me < EARLY

    @pl.when(early)
    def _():
        for part in range(2):
            if part == 0:
                rims()
            for s in ACROSS_OFFSETS:
                window(EARLY + (me + s) % EARLY, part)
            for s in GROUP_OFFSETS:
                window((me + s) % EARLY, part)

    @pl.when(jnp.logical_not(early))
    def _():
        for part in range(2):
            for s in GROUP_OFFSETS:
                window(EARLY + (me + s) % EARLY, part)
            if part == 0:
                rims()
            for s in ACROSS_OFFSETS:
                window((me + s) % EARLY, part)

    got[me] = extw[pl.ds(patch_row, 3), patch_col]

    border_row = jnp.where(band == 0, 2, 0)
    other_row = jnp.where(band == 0, 0, 3)
    sides = ((0, 0, at_left, col > 0), (1, 3, at_right, col < 7))

    def take(kind, wanted):
        @pl.when(wanted)
        def _():
            pltpu.make_async_copy(halo.at[kind], halo.at[kind], h_recv.at[kind]).wait()
            for f in range(FRAMES):
                gh[kind, 4 * f : 4 * f + 4] = halo[kind, f].astype(F32)

    def arrive(part):
        lo, hi = PARTS[part]
        block = got.at[pl.ds(0, 31), lo:hi]
        pltpu.make_async_copy(block, block, in_recv.at[part]).wait()
        for f in range(FRAMES):
            for k in range(lo, hi):
                gf[12 * f + 4 * k : 12 * f + 4 * k + 4] = got[f, k].astype(F32)
        has_border = at_border & (band == 1 - part)

        @pl.when(has_border)
        def _():
            for c in range(4):
                gf[pl.ds(4 * border_row + c, FRAMES, stride=12)] = gh[
                    2, pl.ds(c, FRAMES, stride=4)
                ]

        for kind, c, at_side, inside in sides:

            @pl.when(at_side & inside)
            def _():
                for k in range(lo, hi):
                    r = jnp.clip(patch_row - 1 + k, 0, 3)
                    gf[pl.ds(4 * k + c, FRAMES, stride=12)] = gh[
                        kind, pl.ds(r, FRAMES, stride=4)
                    ]

            @pl.when(at_side & inside & has_border)
            def _():
                gf[pl.ds(4 * border_row + c, FRAMES, stride=12)] = gh[
                    kind + 3, pl.ds(other_row, FRAMES, stride=4)
                ]

    keep_top = jnp.where((band == 0) & (patch_row == 0), 0.0, 1.0).astype(F32)
    keep_bottom = jnp.where((band == 1) & (patch_row == 3), 0.0, 1.0).astype(F32)
    keep_left = jnp.where((col == 0) & at_left, 0.0, 1.0).astype(F32)
    keep_right = jnp.where((col == 7) & at_right, 0.0, 1.0).astype(F32)
    def lift(k, lines):
        two = [[gf[pl.ds(4 * i + c, FRAMES, stride=12)] for c in range(4)] for i in (k, k + 1)]
        for y, taps in lines:
            row = spread([lerp(taps, two[0][c], two[1][c]) for c in range(4)])
            for x in range(10):
                value = row[x]
                if y == 0:
                    value = value * keep_top
                if y == 5:
                    value = value * keep_bottom
                if x == 0:
                    value = value * keep_left
                if x == 9:
                    value = value * keep_right
                u[y, x] = value.astype(BF16)

    take(0, at_left)
    take(1, at_right)
    take(2, at_border)
    take(3, at_border & at_left)
    take(4, at_border & at_right)
    arrive(0)
    lift(0, ((0, TAPS[3]), (1, TAPS[0]), (2, TAPS[1])))

    load_w.wait()
    load_ain.wait()
    load_aout.wait()

    lane = lax.broadcasted_iota(jnp.int32, (128, CH), 1)
    head0 = (lane < 64).astype(F32).astype(BF16)
    head1 = (lane >= 64).astype(F32).astype(BF16)
    ones = jnp.concatenate([head0, head1], axis=0)
    s_row = lax.broadcasted_iota(jnp.int32, (128, 256), 0) // FRAMES
    s_lane = lax.broadcasted_iota(jnp.int32, (128, 256), 1) % 128 // FRAMES
    same_pixel = s_row == s_lane

    def give(h, frame):
        top, bottom = PIECES[h]

        @pl.when(frame != me)
        def _():
            pltpu.make_async_remote_copy(
                src_ref=snd.at[frame, top:bottom], dst_ref=out.at[patch, top:bottom],
                send_sem=o_send.at[h], recv_sem=o_recv.at[h],
                device_id=(base + frame, col), device_id_type=MESH,
            ).start()

    own = []
    for h, (top, bottom) in enumerate(PIECES):
        if h == 1:
            arrive(1)
            lift(1, ((3, TAPS[2]), (4, TAPS[3]), (5, TAPS[0])))
        pixels = 8 * (bottom - top)
        rows = pixels * FRAMES
        frame_id = lax.broadcasted_iota(jnp.int32, (rows, CH), 0) % FRAMES
        lhs = jnp.concatenate(
            [
                u[top + dy : bottom + dy, dx : dx + 8].reshape(rows, CH)
                for dy in range(3)
                for dx in range(3)
            ],
            axis=1,
        )
        w01 = jnp.concatenate([w[0:1152], w[1152:2304]], axis=1)
        y01 = jnp.dot(lhs, w01, preferred_element_type=F32)
        y2 = jnp.dot(lhs, w[2304:3456], preferred_element_type=F32)
        before = jnp.where(frame_id == 0, 0.0, pltpu.roll(y01[:, :CH], 1, 0))
        after = jnp.where(frame_id == FRAMES - 1, 0.0, pltpu.roll(y2, rows - 1, 0))
        total = before + y01[:, CH:] + after
        centre = u[top + 1 : bottom + 1, 1:9].reshape(rows, CH).astype(F32)
        feat = (centre + total / (1.0 + jnp.exp(-total))).astype(BF16)
        proj = jnp.dot(feat, ain[...], preferred_element_type=F32).astype(BF16)
        for g in range(rows // 128):
            part = proj[128 * g : 128 * g + 128]
            q = part[:, :CH]
            k = part[:, CH : 2 * CH]
            v = part[:, 2 * CH :]
            keys = jnp.concatenate([k * head0, k * head1], axis=0)
            scores = lax.dot_general(
                q, keys, (((1,), (1,)), ((), ())), preferred_element_type=F32
            )
            scores = jnp.where(same_pixel, scores * 0.125, -1e30)
            m0 = jnp.max(scores[:, :128], axis=1, keepdims=True)
            m1 = jnp.max(scores[:, 128:], axis=1, keepdims=True)
            expo = jnp.concatenate(
                [jnp.exp(scores[:, :128] - m0), jnp.exp(scores[:, 128:] - m1)], axis=1
            ).astype(BF16)
            values = jnp.concatenate([v * head0, v * head1], axis=0)
            summed = jnp.dot(
                expo, jnp.concatenate([values, ones], axis=1), preferred_element_type=F32
            )
            context = (summed[:, :CH] / summed[:, CH:]).astype(BF16)
            output = jnp.dot(context, aout[...], preferred_element_type=F32)
            rf[128 * g : 128 * g + 128] = feat[128 * g : 128 * g + 128].astype(F32) + output
        for f in range(FRAMES):
            for y in range(bottom - top):
                snd[f, top + y] = rf[pl.ds(256 * y + f, 8, stride=FRAMES)].astype(BF16)
        for lo in (0, EARLY):
            for s in range(EARLY):
                give(h, lo + (me + 15 + s) % EARLY)
        own.append(load(4 + h, snd.at[me, top:bottom], out.at[patch, top:bottom]))

    sent = halo.at[0, pl.ds(0, 18)]
    pltpu.make_async_copy(sent, sent, h_send).wait()
    pltpu.make_async_copy(got.at[pl.ds(0, 31)], got.at[pl.ds(0, 31)], in_send).wait()
    for h, (top, bottom) in enumerate(PIECES):
        block = snd.at[pl.ds(0, 31), top:bottom]
        pltpu.make_async_copy(block, block, o_send.at[h]).wait()
        pltpu.make_async_copy(block, block, o_recv.at[h]).wait()
        own[h].wait()


def local(low_frames, conv_weight, attn_in, attn_out):
    vmem = pltpu.VMEM
    dma = pltpu.SemaphoreType.DMA
    patches = pl.pallas_call(
        kernel,
        out_shape=jax.ShapeDtypeStruct((FRAMES, 4, 8, CH), BF16),
        in_specs=[pl.BlockSpec(memory_space=pl.ANY)] * 4,
        out_specs=pl.BlockSpec(memory_space=pl.ANY),
        scratch_shapes=[
            vmem((4, 16, CH), BF16),
            vmem((27 * CH, CH), BF16),
            vmem((CH, 3 * CH), BF16),
            vmem((CH, CH), BF16),
            vmem((2, 4, CH), BF16),
            vmem((6, 24, CH), F32),
            vmem((6, 8, 4, CH), BF16),
            vmem((FRAMES, 3, 4, CH), BF16),
            vmem((5, FRAMES, 4, CH), BF16),
            vmem((FRAMES * 12 + 16, CH), F32),
            vmem((5, FRAMES * 4 + 8, CH), F32),
            vmem((6, 10, FRAMES, CH), BF16),
            vmem((33 * FRAMES, CH), F32),
            vmem((FRAMES, 4, 8, CH), BF16),
            dma((4 + len(PIECES),)),
            dma,
            dma((2,)),
            dma,
            dma((5,)),
            dma((len(PIECES),)),
            dma((len(PIECES),)),
        ],
        compiler_params=pltpu.CompilerParams(
            collective_id=0, has_side_effects=True, vmem_limit_bytes=56 * 1024 * 1024
        ),
    )(low_frames, conv_weight, attn_in, attn_out)
    blocks = patches.reshape(4, 8, 4, 8, CH)
    return jnp.transpose(blocks, (0, 2, 1, 3, 4)).reshape(16, 64, CH)


def solution(mesh):
    in_specs = (P("rows", "cols", None), P(), P(), P())
    out_specs = P("rows", "cols", None)
    return jax.shard_map(local, mesh=mesh, in_specs=in_specs, out_specs=out_specs, check_vma=False)
```

```python
import jax
import jax.numpy as jnp
from jax import lax
from jax.experimental import pallas as pl
from jax.experimental.pallas import tpu as pltpu
from jax.sharding import PartitionSpec as P

MESH = pl.DeviceIdType.MESH
F32 = jnp.float32
BF16 = jnp.bfloat16
FRAMES = 32
EARLY = 16
GROUP_OFFSETS = [s for d in range(8, 0, -1) for s in ((d,) if d == 8 else (d, 16 - d))]
ACROSS_OFFSETS = [0] + GROUP_OFFSETS[::-1]
CH = 128
PARTS = ((0, 2), (2, 3))
PIECES = ((0, 1), (1, 4))
OFFSETS = [s for d in range(16, 0, -1) for s in ((d,) if d == 16 else (d, 32 - d))]
TAPS = ((0.375, 0.625), (0.125, 0.875), (0.875, 0.125), (0.625, 0.375))


def lerp(weights, a, b):
    return weights[0] * a + weights[1] * b


def spread(x):
    out = [lerp(TAPS[3], x[0], x[1])]
    for k in range(1, len(x) - 1):
        out.append(lerp(TAPS[0], x[k - 1], x[k]))
        out.append(lerp(TAPS[1], x[k - 1], x[k]))
        out.append(lerp(TAPS[2], x[k], x[k + 1]))
        out.append(lerp(TAPS[3], x[k], x[k + 1]))
    out.append(lerp(TAPS[0], x[-2], x[-1]))
    return out


def patch_of(index, band):
    rest = index - 14
    depth = jnp.where(
        index < 8, 0, jnp.where(index < 14, 1 + (index - 8) // 2, 1 + rest // 6)
    )
    column = jnp.where(
        index < 8, index, jnp.where(index < 14, 7 * (index % 2), 1 + rest % 6)
    )
    return jnp.where(band == 0, 3 - depth, depth), column


def kernel(
    low_hbm, w_hbm, ain_hbm, aout_hbm, out,
    low, w, ain, aout, edge, ext, extw, got, halo, gf, gh, u, rf, snd,
    ld_sem, in_send, in_recv, h_send, h_recv, o_send, o_recv,
):
    place = lax.axis_index("rows")
    col = lax.axis_index("cols")
    band = place // FRAMES
    me = place % FRAMES
    base = band * FRAMES
    across = (1 - band) * FRAMES
    left = (col + 7) % 8
    right = (col + 1) % 8
    patch_row, patch_col = patch_of(me, band)
    patch = patch_row * 8 + patch_col
    border = jnp.where(band == 0, 3, 0)
    at_border = patch_row == border
    at_left = patch_col == 0
    at_right = patch_col == 7

    def load(k, src, dst):
        cp = pltpu.make_async_copy(src, dst, ld_sem.at[k])
        cp.start()
        return cp

    load_low = load(0, low_hbm, low)

    bar = pltpu.get_barrier_semaphore()

    def tell(row, column):
        pl.semaphore_signal(bar, inc=1, device_id=(row, column), device_id_type=MESH)

    def tell_ring(ring, column):
        def one(f, _):
            tell(ring + f, column)
            return _

        lax.fori_loop(0, FRAMES, one, 0)

    for s in OFFSETS:
        tell(base + (me + s) % FRAMES, col)

    @pl.when(at_left)
    def _():
        tell_ring(base, left)

    @pl.when(at_right)
    def _():
        tell_ring(base, right)

    @pl.when(at_border)
    def _():
        tell_ring(across, col)

    @pl.when(at_border & at_left)
    def _():
        tell_ring(across, left)

    @pl.when(at_border & at_right)
    def _():
        tell_ring(across, right)

    load_low.wait()
    mine = low[...].astype(F32)
    edge[0] = low[:, 0, :]
    edge[1] = low[:, 15, :]
    ext[1:5, 1:17] = mine
    ext[1:5, 0:1] = mine[:, 0:1]
    ext[1:5, 17:18] = mine[:, 15:16]
    ext[0] = ext[1]
    ext[5] = ext[4]
    for j in range(8):
        extw[:, j] = ext[:, 2 * j : 2 * j + 4].astype(BF16)
    pl.semaphore_wait(bar, FRAMES - 1 + 18)

    def window(to, part):
        lo, hi = PARTS[part]
        r, j = patch_of(to, band)
        pltpu.make_async_remote_copy(
            src_ref=extw.at[pl.ds(r + lo, hi - lo), j], dst_ref=got.at[me, lo:hi],
            send_sem=in_send, recv_sem=in_recv.at[part],
            device_id=(base + to, col), device_id_type=MESH,
        ).start()

    def rim(src, kind, to, column):
        pltpu.make_async_remote_copy(
            src_ref=src, dst_ref=halo.at[kind, me], send_sem=h_send, recv_sem=h_recv.at[kind],
            device_id=(to, column), device_id_type=MESH,
        ).start()

    def rims():
        for to in (0, 8, 10, 12):
            rim(edge.at[1], 0, base + to, right)
        for to in (7, 9, 11, 13):
            rim(edge.at[0], 1, base + to, left)
        for to in range(8):
            rim(extw.at[border + 1, to], 2, across + to, col)
        rim(edge.at[1], 3, across, right)
        rim(edge.at[0], 4, across + 7, left)

    early = me < EARLY

    @pl.when(early)
    def _():
        for part in range(2):
            if part == 0:
                rims()
            for s in ACROSS_OFFSETS:
                window(EARLY + (me + s) % EARLY, part)
            for s in GROUP_OFFSETS:
                window((me + s) % EARLY, part)

    @pl.when(jnp.logical_not(early))
    def _():
        for part in range(2):
            for s in GROUP_OFFSETS:
                window(EARLY + (me + s) % EARLY, part)
            if part == 0:
                rims()
            for s in ACROSS_OFFSETS:
                window((me + s) % EARLY, part)

    load_w = load(1, w_hbm, w)
    load_ain = load(2, ain_hbm, ain)
    load_aout = load(3, aout_hbm, aout)
    got[me] = extw[pl.ds(patch_row, 3), patch_col]

    border_row = jnp.where(band == 0, 2, 0)
    other_row = jnp.where(band == 0, 0, 3)
    sides = ((0, 0, at_left, col > 0), (1, 3, at_right, col < 7))

    def take(kind, wanted):
        @pl.when(wanted)
        def _():
            pltpu.make_async_copy(halo.at[kind], halo.at[kind], h_recv.at[kind]).wait()
            for f in range(FRAMES):
                gh[kind, 4 * f : 4 * f + 4] = halo[kind, f].astype(F32)

    def arrive(part):
        lo, hi = PARTS[part]
        block = got.at[pl.ds(0, 31), lo:hi]
        pltpu.make_async_copy(block, block, in_recv.at[part]).wait()
        for f in range(FRAMES):
            for k in range(lo, hi):
                gf[12 * f + 4 * k : 12 * f + 4 * k + 4] = got[f, k].astype(F32)
        has_border = at_border & (band == 1 - part)

        @pl.when(has_border)
        def _():
            for c in range(4):
                gf[pl.ds(4 * border_row + c, FRAMES, stride=12)] = gh[
                    2, pl.ds(c, FRAMES, stride=4)
                ]

        for kind, c, at_side, inside in sides:

            @pl.when(at_side & inside)
            def _():
                for k in range(lo, hi):
                    r = jnp.clip(patch_row - 1 + k, 0, 3)
                    gf[pl.ds(4 * k + c, FRAMES, stride=12)] = gh[
                        kind, pl.ds(r, FRAMES, stride=4)
                    ]

            @pl.when(at_side & inside & has_border)
            def _():
                gf[pl.ds(4 * border_row + c, FRAMES, stride=12)] = gh[
                    kind + 3, pl.ds(other_row, FRAMES, stride=4)
                ]

    keep_top = jnp.where((band == 0) & (patch_row == 0), 0.0, 1.0).astype(F32)
    keep_bottom = jnp.where((band == 1) & (patch_row == 3), 0.0, 1.0).astype(F32)
    keep_left = jnp.where((col == 0) & at_left, 0.0, 1.0).astype(F32)
    keep_right = jnp.where((col == 7) & at_right, 0.0, 1.0).astype(F32)
    def lift(k, lines):
        two = [[gf[pl.ds(4 * i + c, FRAMES, stride=12)] for c in range(4)] for i in (k, k + 1)]
        for y, taps in lines:
            row = spread([lerp(taps, two[0][c], two[1][c]) for c in range(4)])
            for x in range(10):
                value = row[x]
                if y == 0:
                    value = value * keep_top
                if y == 5:
                    value = value * keep_bottom
                if x == 0:
                    value = value * keep_left
                if x == 9:
                    value = value * keep_right
                u[y, x] = value.astype(BF16)

    take(0, at_left)
    take(1, at_right)
    take(2, at_border)
    take(3, at_border & at_left)
    take(4, at_border & at_right)
    arrive(0)
    lift(0, ((0, TAPS[3]), (1, TAPS[0]), (2, TAPS[1])))

    load_w.wait()
    load_ain.wait()
    load_aout.wait()

    lane = lax.broadcasted_iota(jnp.int32, (128, CH), 1)
    head0 = (lane < 64).astype(F32).astype(BF16)
    head1 = (lane >= 64).astype(F32).astype(BF16)
    ones = jnp.concatenate([head0, head1], axis=0)
    s_row = lax.broadcasted_iota(jnp.int32, (128, 256), 0) // FRAMES
    s_lane = lax.broadcasted_iota(jnp.int32, (128, 256), 1) % 128 // FRAMES
    same_pixel = s_row == s_lane

    def give(h, frame):
        top, bottom = PIECES[h]

        @pl.when(frame != me)
        def _():
            pltpu.make_async_remote_copy(
                src_ref=snd.at[frame, top:bottom], dst_ref=out.at[patch, top:bottom],
                send_sem=o_send.at[h], recv_sem=o_recv.at[h],
                device_id=(base + frame, col), device_id_type=MESH,
            ).start()

    own = []
    for h, (top, bottom) in enumerate(PIECES):
        if h == 1:
            arrive(1)
            lift(1, ((3, TAPS[2]), (4, TAPS[3]), (5, TAPS[0])))
        pixels = 8 * (bottom - top)
        rows = pixels * FRAMES
        frame_id = lax.broadcasted_iota(jnp.int32, (rows, CH), 0) % FRAMES
        lhs = jnp.concatenate(
            [
                u[top + dy : bottom + dy, dx : dx + 8].reshape(rows, CH)
                for dy in range(3)
                for dx in range(3)
            ],
            axis=1,
        )
        w01 = jnp.concatenate([w[0:1152], w[1152:2304]], axis=1)
        y01 = jnp.dot(lhs, w01, preferred_element_type=F32)
        y2 = jnp.dot(lhs, w[2304:3456], preferred_element_type=F32)
        before = jnp.where(frame_id == 0, 0.0, pltpu.roll(y01[:, :CH], 1, 0))
        after = jnp.where(frame_id == FRAMES - 1, 0.0, pltpu.roll(y2, rows - 1, 0))
        total = before + y01[:, CH:] + after
        centre = u[top + 1 : bottom + 1, 1:9].reshape(rows, CH).astype(F32)
        feat = (centre + total / (1.0 + jnp.exp(-total))).astype(BF16)
        proj = jnp.dot(feat, ain[...], preferred_element_type=F32).astype(BF16)
        for g in range(rows // 128):
            part = proj[128 * g : 128 * g + 128]
            q = part[:, :CH]
            k = part[:, CH : 2 * CH]
            v = part[:, 2 * CH :]
            keys = jnp.concatenate([k * head0, k * head1], axis=0)
            scores = lax.dot_general(
                q, keys, (((1,), (1,)), ((), ())), preferred_element_type=F32
            )
            scores = jnp.where(same_pixel, scores * 0.125, -1e30)
            m0 = jnp.max(scores[:, :128], axis=1, keepdims=True)
            m1 = jnp.max(scores[:, 128:], axis=1, keepdims=True)
            expo = jnp.concatenate(
                [jnp.exp(scores[:, :128] - m0), jnp.exp(scores[:, 128:] - m1)], axis=1
            ).astype(BF16)
            values = jnp.concatenate([v * head0, v * head1], axis=0)
            summed = jnp.dot(
                expo, jnp.concatenate([values, ones], axis=1), preferred_element_type=F32
            )
            context = (summed[:, :CH] / summed[:, CH:]).astype(BF16)
            output = jnp.dot(context, aout[...], preferred_element_type=F32)
            rf[128 * g : 128 * g + 128] = feat[128 * g : 128 * g + 128].astype(F32) + output
        for f in range(FRAMES):
            for y in range(bottom - top):
                snd[f, top + y] = rf[pl.ds(256 * y + f, 8, stride=FRAMES)].astype(BF16)
        for lo in (0, EARLY):
            for s in range(EARLY):
                give(h, lo + (me + 15 + s) % EARLY)
        own.append(load(4 + h, snd.at[me, top:bottom], out.at[patch, top:bottom]))

    sent = halo.at[0, pl.ds(0, 18)]
    pltpu.make_async_copy(sent, sent, h_send).wait()
    pltpu.make_async_copy(got.at[pl.ds(0, 31)], got.at[pl.ds(0, 31)], in_send).wait()
    for h, (top, bottom) in enumerate(PIECES):
        block = snd.at[pl.ds(0, 31), top:bottom]
        pltpu.make_async_copy(block, block, o_send.at[h]).wait()
        pltpu.make_async_copy(block, block, o_recv.at[h]).wait()
        own[h].wait()


def local(low_frames, conv_weight, attn_in, attn_out):
    vmem = pltpu.VMEM
    dma = pltpu.SemaphoreType.DMA
    patches = pl.pallas_call(
        kernel,
        out_shape=jax.ShapeDtypeStruct((FRAMES, 4, 8, CH), BF16),
        in_specs=[pl.BlockSpec(memory_space=pl.ANY)] * 4,
        out_specs=pl.BlockSpec(memory_space=pl.ANY),
        scratch_shapes=[
            vmem((4, 16, CH), BF16),
            vmem((27 * CH, CH), BF16),
            vmem((CH, 3 * CH), BF16),
            vmem((CH, CH), BF16),
            vmem((2, 4, CH), BF16),
            vmem((6, 24, CH), F32),
            vmem((6, 8, 4, CH), BF16),
            vmem((FRAMES, 3, 4, CH), BF16),
            vmem((5, FRAMES, 4, CH), BF16),
            vmem((FRAMES * 12 + 16, CH), F32),
            vmem((5, FRAMES * 4 + 8, CH), F32),
            vmem((6, 10, FRAMES, CH), BF16),
            vmem((33 * FRAMES, CH), F32),
            vmem((FRAMES, 4, 8, CH), BF16),
            dma((4 + len(PIECES),)),
            dma,
            dma((2,)),
            dma,
            dma((5,)),
            dma((len(PIECES),)),
            dma((len(PIECES),)),
        ],
        compiler_params=pltpu.CompilerParams(
            collective_id=0, has_side_effects=True, vmem_limit_bytes=56 * 1024 * 1024
        ),
    )(low_frames, conv_weight, attn_in, attn_out)
    blocks = patches.reshape(4, 8, 4, 8, CH)
    return jnp.transpose(blocks, (0, 2, 1, 3, 4)).reshape(16, 64, CH)


def solution(mesh):
    in_specs = (P("rows", "cols", None), P(), P(), P())
    out_specs = P("rows", "cols", None)
    return jax.shard_map(local, mesh=mesh, in_specs=in_specs, out_specs=out_specs, check_vma=False)
```
